128 devices in a mesh: role: 2 (over y_hi), vocab: 64 (over x, y_lo, z, core).
Axes of the slice: x: 4, y: 4 (y_hi: 2, y_lo: 2; y = y_hi * 2 + y_lo), z: 4, core: 2. Of those that a mesh axis runs over, the one named last changes fastest.
Arguments:
- teacher_hidden: bfloat16 [256, 16384], P('role', 'vocab'), may hold values from -600 to 600
- teacher_gain: bfloat16 [16384], replicated, may hold values from 0.25 to 1.75
- teacher_head: bfloat16 [65536, 16384], P(('role', 'vocab')), may hold values from -0.3125 to 0.3125
- student_hidden: bfloat16 [256, 4096], P(('role', 'vocab')), may hold values from -600 to 600
- student_gain: bfloat16 [4096], replicated, may hold values from 0.25 to 1.75
- student_head: bfloat16 [65536, 4096], P(('role', 'vocab')), may hold values from -0.625 to 0.625
- token_ids: int32 [256], replicated, may hold values from 0 to 65535
- teacher_map: int32 [128], replicated, may hold values from 0 to 127, each once
- student_map: int32 [128], replicated, may hold values from 0 to 127, each once
Outputs:
- loss: float32 [], replicated
- head_grad: bfloat16 [65536, 4096], P(('role', 'vocab'))
- input_grad: float32 [256, 4096], P(('role', 'vocab'))
The draws below stay inside these ranges and needn't reach their ends.
Inputs may be any that keep to these rules, and one draw needn't show every extreme that they name: A permutation: each of the 128 vocabulary blocks once; rows i * 512 to (i + 1) * 512 - 1 of teacher_head belong to vocabulary block teacher_map[i]. A permutation: each of the 128 vocabulary blocks once; rows i * 512 to (i + 1) * 512 - 1 of student_head belong to vocabulary block student_map[i].
All inputs are finite; a program needn't handle non-finite values.
Results may differ from the reference program's by a relative error of at most 0.0095.
The reference program's roundings to bfloat16 on the way count: a program that leaves them out, or rounds other values in their place, can miss the bound.
Values may be sent and summed in bfloat16 or wider, within the bound.
A program may use at most 128 MiB of HBM per device.

```python
import math
import jax
import jax.numpy as jnp
import numpy as np
from jax import lax

DS = 4096
DT = 16384
V = 65536
TOKENS = 256
NBLK = 128


def shared_parts(key, label, width):
    base = jax.random.fold_in(key, label)
    scales = jnp.exp(jax.random.uniform(jax.random.fold_in(base, 1), (width,), jnp.float32, 0.0, math.log(10.0)))
    return scales


def tilted(scales, top):
    steps = jnp.arange(TOKENS, dtype=jnp.float32) / max(TOKENS - 1, 1)
    tilt = top * steps
    return jnp.exp(tilt[:, None] * jnp.log(scales / math.sqrt(10.0))[None, :])


def hidden_rows(key, scales, width):
    row_scale = jnp.exp(jax.random.uniform(jax.random.fold_in(key, 1), (TOKENS,), jnp.float32, 0.0, math.log(10.0)))
    base = jnp.clip(jax.random.normal(jax.random.fold_in(key, 2), (TOKENS, width), jnp.float32), -5.9, 5.9)
    rows = base * tilted(scales, 2.0)
    return (rows * row_scale[:, None]).astype(jnp.bfloat16)


def head_rows(key, scales, width):
    spread = 3.0 / math.sqrt(width)
    columns = (scales / 4.64)[None, :]
    head = jnp.clip(jax.random.normal(key, (V, width), jnp.float32), -6.0, 6.0) * spread * columns
    return head.astype(jnp.bfloat16)


def draw_teacher_hidden(key, part):
    scales = shared_parts(key, 11, DT)
    key = jax.random.fold_in(key, 1)
    return hidden_rows(key, scales, DT)


def draw_teacher_head(key, part):
    scales = shared_parts(key, 11, DT)
    key = jax.random.fold_in(key, 2)
    return head_rows(key, scales, DT)


def draw_student_hidden(key, part):
    scales = shared_parts(key, 23, DS)
    key = jax.random.fold_in(key, 3)
    return hidden_rows(key, scales, DS)


def draw_student_head(key, part):
    scales = shared_parts(key, 23, DS)
    key = jax.random.fold_in(key, 4)
    return head_rows(key, scales, DS)


def plant(result, rng, least, top_value):
    longest = result.shape.index(max(result.shape))
    spots = []
    for shift in (0, 1):
        where = [jax.random.randint(jax.random.fold_in(rng, axis), (), 0, length) for axis, length in enumerate(result.shape)]
        where[longest] = (where[longest] + shift) % result.shape[longest]
        spots.append(tuple(where))
    return result.at[spots[0]].set(least).at[spots[1]].set(top_value)


def cumulative_ranks(amount, slope):
    loads = [(1 << 20) // math.isqrt(standing ** slope) + 1 for standing in range(1, amount + 1)]
    scale = 1 + sum(loads) // (1 << 30)
    return np.cumsum(np.array([max(1, weight // scale) for weight in loads]))


def skewed_ids(key, shape, amount, lean):
    grid = cumulative_ranks(amount, lean)
    lot = jax.random.randint(jax.random.fold_in(key, 1), shape, 0, int(grid[amount - 1]))
    rank = jnp.searchsorted(jnp.asarray(grid, jnp.int32), lot, side="right")
    return jax.random.permutation(jax.random.fold_in(key, 2), amount)[rank].astype(jnp.int32)


def setup_inputs(seed: int = 0) -> dict:
    splits = jax.random.split(jax.random.key(seed), 10)
    return {
        "teacher_hidden": draw_teacher_hidden(jax.random.fold_in(splits[9], 71), 0),
        "teacher_gain": jnp.clip(1.0 + 0.15 * jax.random.normal(splits[1], (DT,), jnp.float32), 0.25, 1.75).astype(jnp.bfloat16),
        "teacher_head": draw_teacher_head(jax.random.fold_in(splits[9], 71), 0),
        "student_hidden": draw_student_hidden(jax.random.fold_in(splits[9], 71), 0),
        "student_gain": jnp.clip(1.0 + 0.15 * jax.random.normal(splits[4], (DS,), jnp.float32), 0.25, 1.75).astype(jnp.bfloat16),
        "student_head": draw_student_head(jax.random.fold_in(splits[9], 71), 0),
        "token_ids": plant(skewed_ids(splits[6], (TOKENS,), V, 2), jax.random.fold_in(splits[6], 3), 0, V - 1).astype(jnp.int32),
        "teacher_map": jax.random.permutation(splits[7], NBLK).astype(jnp.int32),
        "student_map": jax.random.permutation(splits[8], NBLK).astype(jnp.int32),
    }


EPS = 1e-05
LOSS_SCALE = 256.0
CE_WEIGHT = 0.25

def normalize(rows, gain):
    rows_f = rows.astype(jnp.float32)
    scale = lax.rsqrt(lax.optimization_barrier(jnp.mean(rows_f * rows_f, axis=-1, keepdims=True)) + EPS)
    return (rows_f * scale * gain.astype(jnp.float32), scale)

def positions(mapping, wanted):
    count = mapping.shape[0]
    match = mapping[None, :] == wanted[:, None]
    return lax.optimization_barrier(jnp.sum(jnp.where(match, jnp.arange(count, dtype=jnp.int32)[None, :], 0), axis=1)).astype(jnp.int32)

def token_terms(teach_vals, stud_vals, label_hit):
    teach_top = lax.optimization_barrier(jnp.max(teach_vals, axis=1, keepdims=True))
    teach_log = teach_top + jnp.log(lax.optimization_barrier(jnp.sum(jnp.exp(teach_vals - teach_top), axis=1, keepdims=True)))
    stud_top = lax.optimization_barrier(jnp.max(stud_vals, axis=1, keepdims=True))
    stud_log = stud_top + jnp.log(lax.optimization_barrier(jnp.sum(jnp.exp(stud_vals - stud_top), axis=1, keepdims=True)))
    teach_prob = jnp.exp(teach_vals - teach_log)
    stud_prob = jnp.exp(stud_vals - stud_log)
    diverge = lax.optimization_barrier(jnp.sum(teach_prob * (teach_vals - stud_vals), axis=1)) - teach_log[:, 0] + stud_log[:, 0]
    picked = lax.optimization_barrier(jnp.sum(jnp.where(label_hit, stud_vals, 0.0), axis=1))
    cross_ent = stud_log[:, 0] - picked
    hit_f = label_hit.astype(jnp.float32)
    grad = (LOSS_SCALE * ((1.0 + CE_WEIGHT) * stud_prob - teach_prob - CE_WEIGHT * hit_f)).astype(jnp.bfloat16)
    return (diverge + CE_WEIGHT * cross_ent, grad)

def reference(teacher_hidden, teacher_gain, teacher_head, student_hidden, student_gain, student_head, token_ids, teacher_map, student_map):
    teacher_normed = normalize(teacher_hidden, teacher_gain)[0].astype(jnp.bfloat16)
    teacher_logits = jnp.dot(teacher_normed, teacher_head.T, preferred_element_type=jnp.float32).astype(jnp.bfloat16)
    stud_norm, stud_scale = normalize(student_hidden, student_gain)
    student_normed = stud_norm.astype(jnp.bfloat16)
    student_logits = jnp.dot(student_normed, student_head.T, preferred_element_type=jnp.float32).astype(jnp.bfloat16)
    nblk = teacher_map.shape[0]
    width = V // nblk
    order = positions(teacher_map, student_map)
    aligned = teacher_logits.reshape(TOKENS, nblk, width)[:, order, :].reshape(TOKENS, V)
    label_col = positions(student_map, (token_ids // width).astype(jnp.int32)) * width + token_ids % width
    label_hit = jnp.arange(V, dtype=jnp.int32)[None, :] == label_col.astype(jnp.int32)[:, None]
    per_token, grad = token_terms(aligned.astype(jnp.float32), student_logits.astype(jnp.float32), label_hit)
    loss = jnp.mean(per_token)
    head_grad = jnp.dot(grad.T, student_normed, preferred_element_type=jnp.float32).astype(jnp.bfloat16)
    hidden_back = jnp.dot(grad, student_head, preferred_element_type=jnp.float32)
    hat = student_hidden.astype(jnp.float32) * stud_scale
    back = hidden_back * student_gain.astype(jnp.float32)
    input_grad = stud_scale * (back - hat * lax.optimization_barrier(jnp.mean(back * hat, axis=1, keepdims=True)))
    return (loss, head_grad, input_grad)
```

```python
import jax
import jax.numpy as jnp
from jax import lax
from jax.experimental import pallas as pl
from jax.experimental.pallas import tpu as pltpu
from jax.sharding import PartitionSpec as P

EPS = 1e-05
LOSS_SCALE = 256.0
CE_WEIGHT = 0.25
MESH = pl.DeviceIdType.MESH
F32 = jnp.float32
BF16 = jnp.bfloat16
X, Y, Z = 0, 1, 2
ALL = pl.ds(0, 4)
PARTS = (((Y, Z, X), 0, 32), ((Z, X, Y), 32, 48), ((X, Y, Z), 80, 48))
N_SEM = 232


def div(a, b):
    return lax.div(a, jnp.int32(b))


def rem(a, b):
    return lax.rem(a, jnp.int32(b))


def flat_of(x, y, z, c):
    return div(y, 2) * 64 + ((x * 2 + rem(y, 2)) * 4 + z) * 2 + c


def shuffle4(tiles, pair):
    out = []
    for b in range(4):
        acc = None
        for a in range(4):
            shift = (2 * (a - b)) % 8
            moved = pltpu.roll(tiles[a], shift, 0) if shift else tiles[a]
            acc = moved if acc is None else jnp.where(pair == a, moved, acc)
        out.append(acc)
    return out


def kernel(
    t_ref,
    tg_ref,
    th_hbm,
    s_ref,
    sg_ref,
    sh_hbm,
    order_ref,
    label_ref,
    loss_ref,
    ig_ref,
    a_out,
    g2_ref,
    gath,
    th,
    sh,
    acc,
    rows_a,
    s_snd,
    s_rcv,
    st_own,
    st_rcv,
    scale_ref,
    tl_snd,
    tl_rcv,
    sl_snd,
    sl_rcv,
    g_snd,
    g_rcv,
    sib_snd,
    sib_rcv,
    hb,
    p1_snd,
    p1_rcv,
    h1,
    p2_snd,
    p2_rcv,
    p3_snd,
    p3_rcv,
    ls_own,
    ls_rcv,
    ssem,
    rsem,
    lsem,
    bulk_s,
    bulk_r,
):
    role = lax.axis_index("role")
    vocab = lax.axis_index("vocab")
    me_c = rem(vocab, 2)
    me = (div(vocab, 16), role * 2 + rem(div(vocab, 8), 2), rem(div(vocab, 2), 4))
    flat = role * 64 + vocab
    j_me = me[X] * 2 + me_c
    g_me = me[Y] * 4 + me[Z]

    def device(x, y, z, c):
        return (div(y, 2), ((x * 2 + rem(y, 2)) * 4 + z) * 2 + c)

    def moved(axis, step):
        return rem(me[axis] + step, 4)

    def line(axis, step):
        at = list(me)
        at[axis] = moved(axis, step)
        return device(at[0], at[1], at[2], me_c)

    sibling = device(me[X], me[Y], me[Z], 1 - me_c)

    def column(k):
        return device(div(k, 2), me[Y], me[Z], rem(k, 2))

    def plane(dy, dz):
        return device(me[X], moved(Y, dy), moved(Z, dz), me_c)

    started = []

    def send(src, dst, to):
        k = len(started)
        copy = pltpu.make_async_remote_copy(
            src, dst, ssem.at[k], rsem.at[k], device_id=to, device_id_type=MESH
        )
        copy.start()
        started.append(copy)
        return copy

    plane_steps = [(dy, dz) for dy in range(4) for dz in range(4) if (dy, dz) != (0, 0)]
    barrier = pltpu.get_barrier_semaphore()
    for k in range(1, 8):
        pl.semaphore_signal(barrier, inc=1, device_id=column(rem(j_me + k, 8)), device_id_type=MESH)
    for dy, dz in plane_steps:
        pl.semaphore_signal(barrier, inc=1, device_id=plane(dy, dz), device_id_type=MESH)

    load_sh = pltpu.make_async_copy(sh_hbm, sh, lsem.at[0])
    load_th = pltpu.make_async_copy(th_hbm, th, lsem.at[1])
    load_sh.start()
    load_th.start()

    own = t_ref[...]
    gath[me[X], me[Y], me[Z], me_c] = own
    own_f = own.astype(F32)
    sums = jnp.sum(own_f * own_f, axis=1, keepdims=True)
    flipped = jnp.broadcast_to(sums, (128, 128)).T[:8]
    st_own[0, 0] = jnp.where(role == 0, flipped, 0.0)
    st_own[0, 1] = jnp.where(role == 1, flipped, 0.0)

    stud = s_ref[...].astype(F32)
    stud_scale = lax.rsqrt(jnp.mean(stud * stud, axis=1, keepdims=True) + EPS)
    stud_normed = (stud * stud_scale * sg_ref[...]).astype(BF16)
    for j in range(8):
        s_snd[j] = stud_normed[:, j * 512 : (j + 1) * 512]
    s_rcv[j_me] = s_snd[j_me]

    pl.semaphore_wait(barrier, 22)

    def at(part, a, b, c):
        (first, second, last), start, count = PARTS[part]
        index = [None, None, None]
        index[first], index[second], index[last] = a, b, c
        return gath.at[index[0], index[1], index[2], me_c, pl.ds(start, count)]

    def axes(part):
        return PARTS[part][0]

    parts = range(3)
    steps = (1, 3, 2)

    first = {}
    for p in parts:
        a, b, c = axes(p)
        mine = at(p, me[a], me[b], me[c])
        for d in steps:
            first[p, d] = send(mine, mine, line(a, d))
    spread = []
    for k in range(1, 8):
        to = rem(j_me + k, 8)
        spread.append(send(s_snd.at[to], s_rcv.at[j_me], column(to)))
    stats = [send(st_own.at[0], st_rcv.at[i], line(X, d)) for i, d in enumerate(steps)]

    heavy = {}
    second = {}
    side = []

    def to_side(ref):
        side.append(send(ref, ref, sibling))

    def start_heavy(p, g):
        a, b, c = axes(p)
        group = at(p, ALL, moved(b, (4 - (0, 1, 3, 2)[g]) % 4), me[c])
        heavy[p, g, 1] = send(group, group, line(c, 1))
        heavy[p, g, 3] = send(group, group, line(c, 3))
        to_side(group)

    for p in parts:
        a, b, c = axes(p)
        for d in steps:
            first[p, d].wait_recv()
        group = at(p, ALL, me[b], me[c])
        for d in steps:
            second[p, d] = send(group, group, line(b, d))
        start_heavy(p, 0)

    for copy in spread:
        copy.wait_recv()
    tile = jnp.concatenate([s_rcv[k].astype(F32) for k in range(8)], axis=0)
    rows_a[j_me, g_me] = tile.astype(BF16)
    tile_ref = rows_a.at[j_me, g_me]
    gather_plane = [send(tile_ref, tile_ref, plane(dy, dz)) for dy, dz in plane_steps]

    def add_stats(stage, copies, base):
        total = st_own[stage]
        for i, copy in enumerate(copies):
            copy.wait_recv()
            total = total + st_rcv[base + i]
        st_own[stage + 1] = total

    add_stats(0, stats, 0)
    stats = [send(st_own.at[1], st_rcv.at[3 + i], line(Y, d)) for i, d in enumerate(steps)]

    for g, d in enumerate(steps):
        for p in parts:
            second[p, d].wait_recv()
            start_heavy(p, g + 1)

    add_stats(1, stats, 3)
    stats = [send(st_own.at[2], st_rcv.at[6 + i], line(Z, d)) for i, d in enumerate(steps)]

    for copy in gather_plane:
        copy.wait_recv()
    chunk_ref = rows_a.at[j_me]
    lines_x = {d: send(chunk_ref, chunk_ref, line(X, d)) for d in steps}
    stud_side = [send(chunk_ref, chunk_ref, sibling)]

    halves = {}
    for g in range(4):
        for p in parts:
            a, b, c = axes(p)
            at_b = moved(b, (4 - (0, 1, 3, 2)[g]) % 4)
            for d, half in ((1, pl.ds(0, 2)), (3, pl.ds(2, 2))):
                heavy[p, g, d].wait_recv()
                from_c = moved(c, 4 - d)
                piece = at(p, half, at_b, from_c)
                halves[p, g, d] = send(piece, piece, line(c, d))
                to_side(at(p, ALL, at_b, from_c))
        if g == 0:
            add_stats(2, stats, 6)
            stats = [send(st_own.at[3], st_rcv.at[9], sibling)]

    for d in steps:
        lines_x[d].wait_recv()
        arrived = rows_a.at[moved(X, 4 - d) * 2 + me_c]
        stud_side.append(send(arrived, arrived, sibling))

    for g in range(4):
        for p in parts:
            a, b, c = axes(p)
            at_b = moved(b, (4 - (0, 1, 3, 2)[g]) % 4)
            for d, half in ((1, pl.ds(0, 2)), (3, pl.ds(2, 2))):
                halves[p, g, d].wait_recv()
                to_side(at(p, half, at_b, moved(c, 2)))

    sub = lax.broadcasted_iota(jnp.int32, (8, 128), 0)
    lane = lax.broadcasted_iota(jnp.int32, (8, 128), 1)
    pair = sub // 2

    def to_owner(out, into, r, index, sem):
        rows = acc[pl.ds(pl.multiple_of(r * 8, 8), 8), :]
        tiles = shuffle4([rows[:, j * 128 : (j + 1) * 128] for j in range(4)], pair)
        for k in range(4):
            to = index(r, k)
            out[to] = tiles[k].astype(BF16)

            @pl.when(to != flat)
            def _():
                pltpu.make_async_remote_copy(
                    out.at[to],
                    into.at[flat],
                    bulk_s.at[sem],
                    bulk_r.at[sem],
                    device_id=(div(to, 64), rem(to, 64)),
                    device_id_type=MESH,
                ).start()

            @pl.when(to == flat)
            def _():
                into[to] = out[to]

    def column_index(r, k):
        g = div(r, 2)
        return flat_of(rem(r, 2) * 2 + k // 2, div(g, 4), rem(g, 4), k % 2)

    def plain_index(r, k):
        return r * 4 + k

    def bulk_wait(buf, sems, sem):
        pltpu.make_async_copy(buf.at[pl.ds(0, 127)], buf.at[pl.ds(0, 127)], sems.at[sem]).wait()

    for copy in stud_side:
        copy.wait_recv()
    load_sh.wait()
    for j in range(8):
        part = lax.dot_general(
            rows_a[j].reshape(256, 512),
            sh[:, j * 512 : (j + 1) * 512],
            (((1,), (1,)), ((), ())),
            preferred_element_type=F32,
        )
        if j == 0:
            acc[...] = part
        else:
            acc[...] += part

    @pl.loop(0, 32)
    def _(i):
        to_owner(sl_snd, sl_rcv, rem(i + g_me * 2, 32), column_index, 0)

    add_stats(3, stats, 9)
    for r in range(2):
        scale = lax.rsqrt(st_own[4, r] * (1.0 / 16384) + EPS)
        scale_ref[r] = jnp.broadcast_to(scale[0:1], (128, 128)).T
    load_th.wait()
    for copy in side:
        copy.wait_recv()
    acc[...] = jnp.zeros_like(acc)

    @pl.loop(0, 16)
    def _(kk):
        x = div(kk, 4)
        y_lo = rem(div(kk, 2), 2)
        z2 = rem(kk, 2) * 2
        lanes = []
        for u in range(4):
            gain = tg_ref[pl.ds(kk, 1), u * 256 : (u + 1) * 256]
            halves_ = []
            for r in range(2):
                block = gath[x, 2 * r + y_lo, z2 + u // 2, u % 2].astype(F32)
                scale = scale_ref[r]
                scale = jnp.concatenate([scale, scale], axis=1)
                halves_.append((block * scale * gain).astype(BF16))
            lanes.append(jnp.concatenate(halves_, axis=0))
        left = jnp.concatenate(lanes, axis=1)
        right = th[:, pl.ds(pl.multiple_of(kk * 1024, 1024), 1024)]
        acc[...] += lax.dot_general(
            left, right, (((1,), (1,)), ((), ())), preferred_element_type=F32
        )

    @pl.loop(0, 32)
    def _(i):
        to_owner(tl_snd, tl_rcv, rem(i + div(flat, 4), 32), plain_index, 1)

    outs = []
    for j in range(8):
        out = pltpu.make_async_copy(
            rows_a.at[j], a_out.at[:, :, pl.ds(j * 512, 512)], lsem.at[2 + j]
        )
        out.start()
        outs.append(out)

    def over(value, op, reduce):
        value = jnp.broadcast_to(reduce(value, axis=1, keepdims=True), (8, 128))
        value = op(value, pltpu.roll(value, 2, 0))
        return op(value, pltpu.roll(value, 4, 0))

    def log_sum(ref):
        def top_step(i, top):
            return jnp.maximum(top, jnp.max(ref[pl.ds(i * 16, 16)].astype(F32), axis=0))

        top = lax.fori_loop(0, 8, top_step, jnp.full((8, 128), -jnp.inf, F32))
        top = over(top, jnp.maximum, jnp.max)

        def sum_step(i, total):
            return total + jnp.sum(jnp.exp(ref[pl.ds(i * 16, 16)].astype(F32) - top[None]), axis=0)

        total = lax.fori_loop(0, 8, sum_step, jnp.zeros((8, 128), F32))
        return top + jnp.log(over(total, jnp.add, jnp.sum))

    bulk_wait(sl_rcv, bulk_r, 0)
    stud_log = log_sum(sl_rcv)
    bulk_wait(tl_rcv, bulk_r, 1)
    teach_log = log_sum(tl_rcv)
    token = sub % 2
    wanted = jnp.where(token == 0, label_ref[flat * 2], label_ref[flat * 2 + 1])
    place = pair * 128 + lane

    def term(n, carry):
        i = rem(n + flat, 128)
        teach = tl_rcv[order_ref[i]].astype(F32)
        student = sl_rcv[i].astype(F32)
        teach_prob = jnp.exp(teach - teach_log)
        stud_prob = jnp.exp(student - stud_log)
        hit = (place + i * 512) == wanted
        grad = LOSS_SCALE * (
            (1.0 + CE_WEIGHT) * stud_prob - teach_prob - CE_WEIGHT * hit.astype(F32)
        )
        g_snd[i] = grad.astype(BF16)

        @pl.when(i != flat)
        def _():
            pltpu.make_async_remote_copy(
                g_snd.at[i],
                g_rcv.at[flat],
                bulk_s.at[2],
                bulk_r.at[2],
                device_id=(div(i, 64), rem(i, 64)),
                device_id_type=MESH,
            ).start()

        return carry + teach_prob * (teach - student) - CE_WEIGHT * jnp.where(hit, student, 0.0)

    total = lax.fori_loop(0, 128, term, jnp.zeros((8, 128), F32), unroll=4)
    g_rcv[flat] = g_snd[flat]
    once = (sub < 2) & (lane == 0)
    total = total + jnp.where(once, (1.0 + CE_WEIGHT) * stud_log - teach_log, 0.0)
    total = jnp.sum(jnp.sum(total, axis=1, keepdims=True), axis=0, keepdims=True)
    ls_own[0] = jnp.broadcast_to(total, (8, 128))
    loss_side = send(ls_own.at[0], ls_rcv.at[0], sibling)

    bulk_wait(g_rcv, bulk_r, 2)

    @pl.loop(0, 16)
    def _(g):
        rows = []
        for h in range(2):
            msgs = [g_rcv[column_index(g * 2 + h, k)].astype(F32) for k in range(4)]
            rows.append(jnp.concatenate(shuffle4(msgs, pair), axis=1))
        start = pl.multiple_of(g * 16, 16)
        g2_ref[pl.ds(start, 16), :] = jnp.concatenate(rows, axis=0).astype(BF16)

    def hidden_cols(core, part):
        cols = pl.ds(pl.multiple_of(core * 2048 + part * 1024, 1024), 1024)
        value = jnp.dot(g2_ref[...], sh[:, cols], preferred_element_type=F32)
        return value.reshape(4, 4, 16, 1024)

    sides = []
    for part in range(2):
        sib_snd[part] = hidden_cols(1 - me_c, part).astype(BF16)
        sides.append(send(sib_snd.at[part], sib_rcv.at[part], sibling))
    for part in range(2):
        hb[part] = hidden_cols(me_c, part)

    def add_loss(stage, copies, base, axis):
        for copy in copies:
            copy.wait_recv()
        total = jnp.zeros((8, 128), F32)
        for i in range(4):
            total = total + jnp.where(me[axis] == i, ls_own[stage], ls_rcv[base + i])
        ls_own[stage + 1] = total

    def spread_loss(stage, base, axis):
        return [
            send(ls_own.at[stage], ls_rcv.at[base + me[axis]], line(axis, d)) for d in steps
        ]

    loss_side.wait_recv()
    ls_own[1] = ls_own[0] + ls_rcv[0]
    for i in range(3):
        ls_rcv[1 + 4 * i + me[(Y, Z, X)[i]]] = jnp.zeros((8, 128), F32)

    phase1 = {}
    for part, axis in enumerate((Y, Z)):
        sides[part].wait_recv()
        summed = hb[part] + sib_rcv[part].astype(F32)
        hb[part] = summed
        p1_snd[part] = (summed if axis == Y else jnp.swapaxes(summed, 0, 1)).astype(BF16)
        for i, d in enumerate(steps):
            phase1[part, i] = send(p1_snd.at[part, moved(axis, d)], p1_rcv.at[part, i], line(axis, d))
    loss_copies = spread_loss(1, 1, Y)

    phase2 = {}
    for part, axis in enumerate((Y, Z)):
        other = (Z, Y)[part]
        total = hb[0, me[Y]] if axis == Y else hb[1, :, me[Z]]
        for i in range(3):
            phase1[part, i].wait_recv()
            total = total + p1_rcv[part, i].astype(F32)
        h1[part] = total
        p2_snd[part] = total.astype(BF16)
        for i, d in enumerate(steps):
            phase2[part, i] = send(p2_snd.at[part, moved(other, d)], p2_rcv.at[part, i], line(other, d))
    add_loss(1, loss_copies, 1, Y)
    loss_copies = spread_loss(2, 5, Z)

    for part in range(2):
        other = (Z, Y)[part]
        total = h1[part, me[other]]
        for i in range(3):
            phase2[part, i].wait_recv()
            total = total + p2_rcv[part, i].astype(F32)
        for k in range(8):
            p3_snd[k, :, part * 1024 : (part + 1) * 1024] = total[2 * k : 2 * k + 2]
    phase3 = []
    for k in range(1, 8):
        to = rem(j_me + k, 8)
        phase3.append(send(p3_snd.at[to], p3_rcv.at[j_me], column(to)))
    p3_rcv[j_me] = p3_snd[j_me]
    add_loss(2, loss_copies, 5, Z)
    loss_copies = spread_loss(3, 9, X)
    for copy in phase3:
        copy.wait_recv()
    back = [
        p3_rcv[c] + p3_rcv[2 + c] + p3_rcv[4 + c] + p3_rcv[6 + c] for c in range(2)
    ]
    back = jnp.concatenate(back, axis=1) * sg_ref[...]
    hat = s_ref[...].astype(F32) * stud_scale
    ig_ref[...] = stud_scale * (back - hat * jnp.mean(back * hat, axis=1, keepdims=True))
    add_loss(3, loss_copies, 9, X)
    loss_ref[...] = ls_own[4] * (1.0 / 256)

    for copy in started:
        copy.wait_send()
    for k, buf in enumerate((sl_snd, tl_snd, g_snd)):
        bulk_wait(buf, bulk_s, k)
    for out in outs:
        out.wait()


def positions(mapping, wanted):
    count = mapping.shape[0]
    match = mapping[None, :] == wanted[:, None]
    return jnp.sum(jnp.where(match, jnp.arange(count, dtype=jnp.int32)[None, :], 0), axis=1)


def body(
    teacher_hidden,
    teacher_gain,
    teacher_head,
    student_hidden,
    student_gain,
    student_head,
    token_ids,
    teacher_map,
    student_map,
):
    order = positions(teacher_map, student_map)
    label_col = positions(student_map, token_ids // 512) * 512 + token_ids % 512
    vmem = pl.BlockSpec(memory_space=pltpu.VMEM)
    smem = pl.BlockSpec(memory_space=pltpu.SMEM)
    hbm = pl.BlockSpec(memory_space=pl.ANY)
    loss, input_grad, rows, grad = pl.pallas_call(
        kernel,
        out_shape=(
            jax.ShapeDtypeStruct((8, 128), F32),
            jax.ShapeDtypeStruct((2, 4096), F32),
            jax.ShapeDtypeStruct((16, 16, 4096), BF16),
            jax.ShapeDtypeStruct((256, 512), BF16),
        ),
        in_specs=[vmem, vmem, hbm, vmem, vmem, hbm, smem, smem],
        out_specs=(vmem, vmem, hbm, vmem),
        scratch_shapes=[
            pltpu.VMEM((4, 4, 4, 2, 128, 256), BF16),
            pltpu.VMEM((512, 16384), BF16),
            pltpu.VMEM((512, 4096), BF16),
            pltpu.VMEM((256, 512), F32),
            pltpu.VMEM((8, 16, 16, 512), BF16),
            pltpu.VMEM((8, 2, 512), BF16),
            pltpu.VMEM((8, 2, 512), BF16),
            pltpu.VMEM((5, 2, 8, 128), F32),
            pltpu.VMEM((10, 2, 8, 128), F32),
            pltpu.VMEM((2, 128, 128), F32),
            pltpu.VMEM((128, 8, 128), BF16),
            pltpu.VMEM((128, 8, 128), BF16),
            pltpu.VMEM((128, 8, 128), BF16),
            pltpu.VMEM((128, 8, 128), BF16),
            pltpu.VMEM((128, 8, 128), BF16),
            pltpu.VMEM((128, 8, 128), BF16),
            pltpu.VMEM((2, 4, 4, 16, 1024), BF16),
            pltpu.VMEM((2, 4, 4, 16, 1024), BF16),
            pltpu.VMEM((2, 4, 4, 16, 1024), F32),
            pltpu.VMEM((2, 4, 4, 16, 1024), BF16),
            pltpu.VMEM((2, 3, 4, 16, 1024), BF16),
            pltpu.VMEM((2, 4, 16, 1024), F32),
            pltpu.VMEM((2, 4, 16, 1024), BF16),
            pltpu.VMEM((2, 3, 16, 1024), BF16),
            pltpu.VMEM((8, 2, 2048), F32),
            pltpu.VMEM((8, 2, 2048), F32),
            pltpu.VMEM((5, 8, 128), F32),
            pltpu.VMEM((13, 8, 128), F32),
            pltpu.SemaphoreType.DMA((N_SEM,)),
            pltpu.SemaphoreType.DMA((N_SEM,)),
            pltpu.SemaphoreType.DMA((10,)),
            pltpu.SemaphoreType.DMA((3,)),
            pltpu.SemaphoreType.DMA((3,)),
        ],
        compiler_params=pltpu.CompilerParams(
            collective_id=0, has_side_effects=True, vmem_limit_bytes=60 << 20
        ),
        cost_estimate=pl.CostEstimate(
            flops=2 * 256 * 512 * (16384 + 2 * 4096), bytes_accessed=24 << 20, transcendentals=0
        ),
        name="distill",
    )(
        teacher_hidden,
        teacher_gain.astype(F32).reshape(16, 1024),
        teacher_head,
        student_hidden,
        student_gain.astype(F32).reshape(1, 4096),
        student_head,
        order,
        label_col,
    )
    head_grad = lax.dot_general(
        grad, rows.reshape(256, 4096), (((0,), (0,)), ((), ())), preferred_element_type=F32
    ).astype(BF16)
    return (loss[0, 0], head_grad, input_grad)


def solution(mesh):
    placed = (
        P("role", "vocab"),
        P(),
        P(("role", "vocab"), None),
        P(("role", "vocab"), None),
        P(),
        P(("role", "vocab"), None),
        P(),
        P(),
        P(),
    )
    return jax.shard_map(
        body,
        mesh=mesh,
        in_specs=placed,
        out_specs=(P(), P(("role", "vocab"), None), P(("role", "vocab"), None)),
        check_vma=False,
    )
```

```python
import jax
import jax.numpy as jnp
from jax import lax
from jax.experimental import pallas as pl
from jax.experimental.pallas import tpu as pltpu
from jax.sharding import PartitionSpec as P

EPS = 1e-05
LOSS_SCALE = 256.0
CE_WEIGHT = 0.25
MESH = pl.DeviceIdType.MESH
F32 = jnp.float32
BF16 = jnp.bfloat16
X, Y, Z = 0, 1, 2
ALL = pl.ds(0, 4)
PARTS = (((Y, Z, X), 0, 32), ((X, Z, Y), 32, 48), ((Y, X, Z), 80, 48))
SEND = {name: k for k, name in enumerate(
    ("spread", "plane", "ring", "stud_side", "first", "second", "last", "side", "stats", "loss", "sib", "line", "direct")
)}
RECV_COUNTS = dict(
    spread=1, plane=1, ring=4, far=1, stud_side=1, first=9, second=9, heavy=24, halves=12,
    side=2, stats=4, loss=4, sib=4, line=4, direct=2,
)
RECV = {name: sum(list(RECV_COUNTS.values())[:k]) for k, name in enumerate(RECV_COUNTS)}
N_RECV = sum(RECV_COUNTS.values())


def div(a, b):
    return lax.div(a, jnp.int32(b))


def rem(a, b):
    return lax.rem(a, jnp.int32(b))


def flat_of(x, y, z, c):
    return div(y, 2) * 64 + ((x * 2 + rem(y, 2)) * 4 + z) * 2 + c


def shuffle4(tiles, pair):
    out = []
    for b in range(4):
        acc = None
        for a in range(4):
            shift = (2 * (a - b)) % 8
            moved = pltpu.roll(tiles[a], shift, 0) if shift else tiles[a]
            acc = moved if acc is None else jnp.where(pair == a, moved, acc)
        out.append(acc)
    return out


def kernel(
    t_hbm,
    tg_hbm,
    th_hbm,
    s_hbm,
    sg_hbm,
    sh_hbm,
    ids_hbm,
    tm_hbm,
    sm_hbm,
    loss_ref,
    ig_ref,
    g2t_out,
    rows_out,
    gath,
    th,
    sh,
    tg,
    sg,
    s_ref,
    tmap,
    smap,
    order_vec,
    ids,
    order_ref,
    acc,
    acc_s,
    rows_a,
    s_snd,
    s_rcv,
    st_own,
    st_rcv,
    scale_ref,
    tl_snd,
    tl_rcv,
    sl_snd,
    sl_rcv,
    g_snd,
    g_rcv,
    g2_ref,
    g2t,
    sib_snd,
    sib_rcv,
    hb,
    p1_snd,
    p1_rcv,
    p2_snd,
    p2_rcv,
    ls_own,
    ls_rcv,
    ssem,
    rsem,
    lsem,
    bulk_s,
    bulk_r,
):
    role = lax.axis_index("role")
    vocab = lax.axis_index("vocab")
    me_c = rem(vocab, 2)
    me = (div(vocab, 16), role * 2 + rem(div(vocab, 8), 2), rem(div(vocab, 2), 4))
    flat = role * 64 + vocab
    j_me = me[X] * 2 + me_c
    g_me = me[Y] * 4 + me[Z]

    def device(x, y, z, c):
        return (div(y, 2), ((x * 2 + rem(y, 2)) * 4 + z) * 2 + c)

    def moved(axis, step):
        return rem(me[axis] + step, 4)

    def line(axis, step):
        at = list(me)
        at[axis] = moved(axis, step)
        return device(at[0], at[1], at[2], me_c)

    sibling = device(me[X], me[Y], me[Z], 1 - me_c)

    def column(k):
        return device(div(k, 2), me[Y], me[Z], rem(k, 2))

    def plane(dy, dz):
        return device(me[X], moved(Y, dy), moved(Z, dz), me_c)

    def send(src, dst, to, group, index=0, sender=None):
        pltpu.make_async_remote_copy(
            src,
            dst,
            ssem.at[SEND[sender or group]],
            rsem.at[RECV[group] + index],
            device_id=to,
            device_id_type=MESH,
        ).start()

    def arrived(ref, group, index=0):
        pltpu.make_async_copy(ref, ref, rsem.at[RECV[group] + index]).wait()

    def left(ref, sender):
        pltpu.make_async_copy(ref, ref, ssem.at[SEND[sender]]).wait()

    plane_steps = [(dy, dz) for dy in range(4) for dz in range(4) if (dy, dz) != (0, 0)]
    barrier = pltpu.get_barrier_semaphore()
    for k in range(1, 8):
        pl.semaphore_signal(barrier, inc=1, device_id=column(rem(j_me + k, 8)), device_id_type=MESH)
    for dy, dz in plane_steps:
        pl.semaphore_signal(barrier, inc=1, device_id=plane(dy, dz), device_id_type=MESH)

    own_slot = gath.at[me[X], me[Y], me[Z], me_c]
    loads = [
        pltpu.make_async_copy(src, dst, lsem.at[k])
        for k, (src, dst) in enumerate(
            (
                (t_hbm, own_slot),
                (s_hbm, s_ref),
                (sg_hbm, sg),
                (tg_hbm, tg),
                (tm_hbm, tmap),
                (sm_hbm, smap),
                (ids_hbm, ids),
                (sh_hbm, sh),
                (th_hbm, th),
            )
        )
    ]
    for load in loads[:7]:
        load.start()
    load_sh, load_th = loads[7:]

    loads[1].wait()
    loads[2].wait()
    stud = s_ref[...].astype(F32)
    stud_gain = sg[...].astype(F32).reshape(1, 4096)
    stud_scale = lax.rsqrt(jnp.mean(stud * stud, axis=1, keepdims=True) + EPS)
    stud_normed = (stud * stud_scale * stud_gain).astype(BF16)
    for j in range(8):
        s_snd[j] = stud_normed[:, j * 512 : (j + 1) * 512]
    s_rcv[j_me] = s_snd[j_me]
    loads[0].wait()

    pl.semaphore_wait(barrier, 22)

    def at(part, a, b, c):
        (first, second, last), start, count = PARTS[part]
        index = [None, None, None]
        index[first], index[second], index[last] = a, b, c
        return gath.at[index[0], index[1], index[2], me_c, pl.ds(start, count)]

    def axes(part):
        return PARTS[part][0]

    parts = range(3)
    steps = (1, 3, 2)

    for k in range(1, 8):
        to = rem(j_me + k, 8)
        send(s_snd.at[to], s_rcv.at[j_me], column(to), "spread")

    def no(p, d):
        return p * 3 + steps.index(d)

    def last_no(p, g, d):
        return (p * 4 + g) * 2 + d // 2

    def mine(p):
        a, b, c = axes(p)
        return at(p, me[a], me[b], me[c])

    for p in parts:
        a, b, c = axes(p)
        for d in steps:
            send(mine(p), mine(p), line(a, d), "first", no(p, d))
    for p in parts:
        a, b, c = axes(p)
        for d in (1, 3):
            send(mine(p), mine(p), line(c, d), "heavy", last_no(p, 0, d), "last")
        for d in steps:
            send(mine(p), mine(p), line(b, d), "second", no(p, d))
    own_f = own_slot[...].astype(F32)
    sums = jnp.sum(own_f * own_f, axis=1, keepdims=True)
    flipped = jnp.broadcast_to(sums, (128, 128)).T[:8]
    st_own[0, 0] = jnp.where(role == 0, flipped, 0.0)
    st_own[0, 1] = jnp.where(role == 1, flipped, 0.0)

    def spread_stats(stage):
        for i, d in enumerate(steps):
            send(st_own.at[stage], st_rcv.at[stage * 3 + i], line((X, Y, Z)[stage], d), "stats", stage)

    def add_stats(stage):
        arrived(st_rcv.at[pl.ds(stage * 3, 3)], "stats", stage)
        total = st_own[stage]
        for i in range(3):
            total = total + st_rcv[stage * 3 + i]
        st_own[stage + 1] = total

    spread_stats(0)

    def to_side(g, ref):
        send(ref, ref, sibling, "side", g // 3)

    def to_stud_side(ref):
        send(ref, ref, sibling, "stud_side")

    def offset_b(p, g):
        return moved(axes(p)[1], (0, 3, 1, 2)[g])

    arrived(s_rcv.at[pl.ds(0, 7)], "spread")
    tile = jnp.concatenate([s_rcv[k].astype(F32) for k in range(8)], axis=0)
    rows_a[j_me, g_me] = tile.astype(BF16)
    tile_ref = rows_a.at[j_me, g_me]
    for dy, dz in plane_steps:
        send(tile_ref, tile_ref, plane(dy, dz), "plane")

    for d in steps:
        for p in parts:
            a, b, c = axes(p)
            block = at(p, moved(a, 4 - d), me[b], me[c])
            arrived(block, "first", no(p, d))
            for e in steps:
                send(block, block, line(b, e), "second", no(p, e))
            for e in (1, 3):
                send(block, block, line(c, e), "heavy", last_no(p, 0, e), "last")
    add_stats(0)
    spread_stats(1)
    for p in parts:
        a, b, c = axes(p)
        to_side(0, at(p, ALL, me[b], me[c]))

    low, high = pl.ds(0, 8), pl.ds(8, 8)
    ways = ((1, low, 0), (3, high, 1), (1, high, 2), (3, low, 3))

    def chunk(step, half=pl.ds(0, 16)):
        return rows_a.at[moved(X, step) * 2 + me_c, half]

    arrived(rows_a.at[j_me, pl.ds(0, 15)], "plane")
    for d, half, n in ways:
        send(chunk(0, half), chunk(0, half), line(X, d), "ring", n)
    to_stud_side(chunk(0))

    for g, d in enumerate(steps):
        for p in parts:
            a, b, c = axes(p)
            group = at(p, ALL, offset_b(p, g + 1), me[c])
            arrived(group, "second", no(p, d))
            for e in (1, 3):
                send(group, group, line(c, e), "heavy", last_no(p, g + 1, e), "last")
            to_side(g + 1, group)
    add_stats(1)
    spread_stats(2)

    for load in loads[7:]:
        load.start()

    for load in loads[3:7]:
        load.wait()
    held = jnp.broadcast_to(tmap[...].astype(F32).reshape(1, 128), (128, 128)).T
    student_map = smap[...].astype(F32).reshape(1, 128)
    down = lax.broadcasted_iota(jnp.int32, (128, 128), 0).astype(F32)
    found = jnp.max(jnp.where(held == student_map, down, 0.0), axis=0, keepdims=True)
    order_vec[...] = jnp.broadcast_to(found, (8, 128)).astype(jnp.int32)
    load_order = pltpu.make_async_copy(order_vec, order_ref, lsem.at[9])
    load_order.start()

    two = ((1, pl.ds(0, 2)), (3, pl.ds(2, 2)))

    def pass_heavy(g):
        for p in parts:
            c = axes(p)[2]
            for d, half in two:
                from_c = moved(c, 4 - d)
                group = at(p, ALL, offset_b(p, g), from_c)
                arrived(group, "heavy", last_no(p, g, d))
                piece = at(p, half, offset_b(p, g), from_c)
                send(piece, piece, line(c, d), "halves", p * 4 + g, "last")
                to_side(g, group)

    def pass_halves(g):
        for p in parts:
            c = axes(p)[2]
            group = at(p, ALL, offset_b(p, g), moved(c, 2))
            arrived(group, "halves", p * 4 + g)
            to_side(g, group)

    pass_heavy(0)
    add_stats(2)
    send(st_own.at[3], st_rcv.at[9], sibling, "stats", 3)
    for d, half, n in ways[:2]:
        piece = chunk(4 - d, half)
        arrived(piece, "ring", n)
        send(piece, piece, line(X, d), "far", 0, "ring")
        to_stud_side(piece)
    pass_heavy(1)
    for d, half, n in ways[2:]:
        piece = chunk(4 - d, half)
        arrived(piece, "ring", n)
        to_stud_side(piece)
    pass_halves(0)
    arrived(chunk(2), "far")
    to_stud_side(chunk(2))
    arrived(st_rcv.at[9], "stats", 3)
    for r in range(2):
        total = st_own[3, r] + st_rcv[9, r]
        scale = lax.rsqrt(total * (1.0 / 16384) + EPS)
        scale_ref[r] = jnp.broadcast_to(scale[0:1], (128, 128)).T
    pass_heavy(2)
    pass_halves(1)

    sub = lax.broadcasted_iota(jnp.int32, (8, 128), 0)
    lane = lax.broadcasted_iota(jnp.int32, (8, 128), 1)
    pair = sub // 2

    def start_bulk(src, dst, to, sem):
        pltpu.make_async_remote_copy(
            src,
            dst,
            bulk_s.at[sem],
            bulk_r.at[sem],
            device_id=(div(to, 64), rem(to, 64)),
            device_id_type=MESH,
        ).start()

    def fill_messages(source, out, r, index):
        rows = source[pl.ds(pl.multiple_of(r * 8, 8), 8), :]
        tiles = shuffle4([rows[:, j * 128 : (j + 1) * 128] for j in range(4)], pair)
        for k in range(4):
            out[index(r, jnp.int32(k))] = tiles[k].astype(BF16)

    def to_owners(source, out, into, own_r, own_k, index, sem, i):
        r = rem(own_r + i, 32)
        fill_messages(source, out, r, index)
        for k in range(4):
            to = index(r, jnp.int32(k))
            start_bulk(out.at[to], into.at[flat], to, sem)

    def to_near_owners(source, out, into, own_r, own_k, index, sem):
        fill_messages(source, out, own_r, index)
        into[flat] = out[flat]
        for i in range(1, 4):
            to = index(own_r, rem(own_k + i, 4))
            start_bulk(out.at[to], into.at[flat], to, sem)

    def column_index(r, k):
        g = div(r, 2)
        return flat_of(rem(r, 2) * 2 + div(k, 2), div(g, 4), rem(g, 4), rem(k, 2))

    def plain_index(r, k):
        return r * 4 + k

    def bulk_wait(buf, sems, sem):
        pltpu.make_async_copy(buf.at[pl.ds(0, 127)], buf.at[pl.ds(0, 127)], sems.at[sem]).wait()

    arrived(rows_a.at[pl.ds(0, 4)], "stud_side")
    load_sh.wait()
    for j in range(8):
        part = lax.dot_general(
            rows_a[j].reshape(256, 512),
            sh[:, j * 512 : (j + 1) * 512],
            (((1,), (1,)), ((), ())),
            preferred_element_type=F32,
        )
        if j == 0:
            acc_s[...] = part
        else:
            acc_s[...] += part
    stud_args = (acc_s, sl_snd, sl_rcv, g_me * 2 + div(me[X], 2), rem(me[X], 2) * 2 + me_c, column_index, 0)
    pass_heavy(3)
    pass_halves(2)
    outs = [pltpu.make_async_copy(rows_a, rows_out, lsem.at[10])]
    outs[0].start()

    load_th.wait()
    arrived(gath.at[pl.ds(0, 3), :, :, 0], "side", 0)
    acc[...] = jnp.zeros_like(acc)

    def teacher_step(dx, dz):
        x, z = rem(me[X] + dx, 4), rem(me[Z] + dz, 4)
        total = None
        for y_lo in range(2):
            base = pl.multiple_of(x * 4096 + y_lo * 2048 + z * 512, 512)
            gain = tg[pl.ds(base, 512)].astype(F32).reshape(1, 512)
            lanes = []
            for c in range(2):
                rows = []
                for r in range(2):
                    block = gath[x, 2 * r + y_lo, z, c].astype(F32)
                    scale = scale_ref[r]
                    scale = jnp.concatenate([scale, scale], axis=1)
                    rows.append((block * scale * gain[:, c * 256 : (c + 1) * 256]).astype(BF16))
                lanes.append(jnp.concatenate(rows, axis=0))
            part = lax.dot_general(
                jnp.concatenate(lanes, axis=1),
                th[:, pl.ds(base, 512)],
                (((1,), (1,)), ((), ())),
                preferred_element_type=F32,
            )
            total = part if total is None else total + part
        acc[...] += total

    @pl.loop(0, 9)
    def _(i):
        q, w = div(i, 3), rem(i, 3)
        for n in range(1, 4):
            to_owners(*stud_args, i * 3 + n)
        teacher_step(q + div(q, 2), w + div(w, 2))

    pass_halves(3)

    @pl.loop(28, 32)
    def _(i):
        to_owners(*stud_args, i)

    to_near_owners(*stud_args)
    arrived(gath.at[0, :, :, 0], "side", 1)

    @pl.loop(0, 4)
    def _(i):
        teacher_step(2, i)

    @pl.loop(0, 3)
    def _(q):
        teacher_step(q + div(q, 2), 2)

    teach_args = (acc, tl_snd, tl_rcv, div(flat, 4), rem(flat, 4), plain_index, 1)

    @pl.loop(1, 32)
    def _(i):
        to_owners(*teach_args, i)

    to_near_owners(*teach_args)

    def over(value, op, reduce):
        value = jnp.broadcast_to(reduce(value, axis=1, keepdims=True), (8, 128))
        value = op(value, pltpu.roll(value, 2, 0))
        return op(value, pltpu.roll(value, 4, 0))

    def log_sum(ref):
        def top_step(i, top):
            return jnp.maximum(top, jnp.max(ref[pl.ds(i * 16, 16)].astype(F32), axis=0))

        top = lax.fori_loop(0, 8, top_step, jnp.full((8, 128), -jnp.inf, F32))
        top = over(top, jnp.maximum, jnp.max)

        def sum_step(i, total):
            return total + jnp.sum(jnp.exp(ref[pl.ds(i * 16, 16)].astype(F32) - top[None]), axis=0)

        total = lax.fori_loop(0, 8, sum_step, jnp.zeros((8, 128), F32))
        return top + jnp.log(over(total, jnp.add, jnp.sum))

    load_order.wait()
    bulk_wait(sl_rcv, bulk_r, 0)
    stud_log = log_sum(sl_rcv)
    bulk_wait(tl_rcv, bulk_r, 1)
    teach_log = log_sum(tl_rcv)
    token = sub % 2
    lane_row = lax.broadcasted_iota(jnp.int32, (1, 128), 1).astype(F32)

    def label_place(label):
        block = div(label, 512)
        match = smap[...].astype(F32).reshape(1, 128) == block.astype(F32)
        place = jnp.sum(jnp.where(match, lane_row, 0.0), axis=1, keepdims=True)
        return place.astype(jnp.int32) * 512 + (label - block * 512)

    wanted = jnp.where(token == 0, label_place(ids[flat * 2]), label_place(ids[flat * 2 + 1]))
    place = pair * 128 + lane

    def term(n, carry):
        i = rem(n + flat, 128)
        teach = tl_rcv[jnp.clip(order_ref[0, i], 0, 127)].astype(F32)
        student = sl_rcv[i].astype(F32)
        teach_prob = jnp.exp(teach - teach_log)
        stud_prob = jnp.exp(student - stud_log)
        hit = (place + i * 512) == wanted
        grad = LOSS_SCALE * (
            (1.0 + CE_WEIGHT) * stud_prob - teach_prob - CE_WEIGHT * hit.astype(F32)
        )
        g_snd[i] = grad.astype(BF16)
        return carry + teach_prob * (teach - student) - CE_WEIGHT * jnp.where(hit, student, 0.0)

    def term_and_send(n, carry):
        carry = term(n, carry)
        i = rem(n + flat, 128)
        start_bulk(g_snd.at[i], g_rcv.at[flat], i, 2)
        return carry

    total = lax.fori_loop(1, 127, term_and_send, jnp.zeros((8, 128), F32), unroll=6)
    total = term_and_send(jnp.int32(127), total)
    total = term(jnp.int32(0), total)
    g_rcv[flat] = g_snd[flat]
    once = (sub < 2) & (lane == 0)
    total = total + jnp.where(once, (1.0 + CE_WEIGHT) * stud_log - teach_log, 0.0)
    total = jnp.sum(jnp.sum(total, axis=1, keepdims=True), axis=0, keepdims=True)
    ls_own[0] = jnp.broadcast_to(total, (8, 128))
    send(ls_own.at[0], ls_rcv.at[0], sibling, "loss", 0)

    def add_loss(stage):
        base = 4 * stage - 3
        axis = (Y, Z, X)[stage - 1]
        arrived(ls_rcv.at[pl.ds(base, 3)], "loss", stage)
        total = jnp.zeros((8, 128), F32)
        for i in range(4):
            total = total + jnp.where(me[axis] == i, ls_own[stage], ls_rcv[base + i])
        ls_own[stage + 1] = total

    def spread_loss(stage):
        base = 4 * stage - 3
        axis = (Y, Z, X)[stage - 1]
        for d in steps:
            send(ls_own.at[stage], ls_rcv.at[base + me[axis]], line(axis, d), "loss", stage)

    for i in range(3):
        ls_rcv[1 + 4 * i + me[(Y, Z, X)[i]]] = jnp.zeros((8, 128), F32)
    arrived(ls_rcv.at[0], "loss", 0)
    ls_own[1] = ls_own[0] + ls_rcv[0]
    spread_loss(1)

    bulk_wait(g_rcv, bulk_r, 2)

    @pl.loop(0, 16)
    def _(g):
        rows = []
        for h in range(2):
            msgs = [g_rcv[column_index(g * 2 + h, k)].astype(F32) for k in range(4)]
            rows.append(jnp.concatenate(shuffle4(msgs, pair), axis=1))
        start = pl.multiple_of(g * 16, 16)
        g2_ref[pl.ds(start, 16), :] = jnp.concatenate(rows, axis=0).astype(BF16)

    def hidden_cols(core, part):
        cols = pl.ds(pl.multiple_of(core * 2048 + part * 512, 512), 512)
        value = jnp.dot(g2_ref[...], sh[:, cols], preferred_element_type=F32)
        return value.reshape(4, 4, 16, 512)

    for part in range(4):
        sib_snd[part] = hidden_cols(1 - me_c, part).astype(BF16)
        send(sib_snd.at[part], sib_rcv.at[part], sibling, "sib", part)
    for part in range(4):
        hb[part] = hidden_cols(me_c, part)
    add_loss(1)
    spread_loss(2)

    for part in range(4):
        axis = (Y, Z)[part % 2]
        arrived(sib_rcv.at[part], "sib", part)
        summed = hb[part] + sib_rcv[part].astype(F32)
        hb[part] = summed
        p1_snd[part] = (summed if axis == Y else jnp.swapaxes(summed, 0, 1)).astype(BF16)
        for i, d in enumerate(steps):
            send(p1_snd.at[part, moved(axis, d)], p1_rcv.at[part, i], line(axis, d), "line", part)

    g2t[...] = g2_ref[...].astype(F32).T.astype(BF16)
    outs.append(pltpu.make_async_copy(g2t, g2t_out, lsem.at[11]))
    outs[1].start()
    add_loss(2)
    spread_loss(3)

    for way, axis in enumerate((Y, Z)):
        for h in range(2):
            part = way + 2 * h
            total = hb[part, me[Y]] if axis == Y else hb[part, :, me[Z]]
            arrived(p1_rcv.at[part], "line", part)
            for i in range(3):
                total = total + p1_rcv[part, i].astype(F32)
            for q in range(4):
                for k in range(8):
                    p2_snd[way, q * 8 + k, :, h * 512 : (h + 1) * 512] = total[q, 2 * k : 2 * k + 2].astype(BF16)
        own = (me[Z] if axis == Y else me[Y]) * 8 + j_me
        p2_rcv[way, own] = p2_snd[way, own]
        for n in range(1, 32):
            to = rem(own + n, 32)
            q, k = div(to, 8), rem(to, 8)
            y, z = (me[Y], q) if axis == Y else (q, me[Z])
            send(
                p2_snd.at[way, to], p2_rcv.at[way, own], device(div(k, 2), y, z, rem(k, 2)), "direct", way
            )
    for way in range(2):
        arrived(p2_rcv.at[way, pl.ds(0, 31)], "direct", way)
    back = []
    for c in range(2):
        sums = []
        for way in range(2):
            total = jnp.zeros((2, 1024), F32)
            for k in range(16):
                total = total + p2_rcv[way, k * 2 + c].astype(F32)
            sums.append(total)
        for part in range(4):
            back.append(sums[part % 2][:, part // 2 * 512 : (part // 2 + 1) * 512])
    back = jnp.concatenate(back, axis=1) * sg[...].astype(F32).reshape(1, 4096)
    hat = s_ref[...].astype(F32) * stud_scale
    ig_ref[...] = stud_scale * (back - hat * jnp.mean(back * hat, axis=1, keepdims=True))
    add_loss(3)
    loss_ref[0, 0] = jnp.sum(jnp.where((sub == 0) & (lane == 0), ls_own[4], 0.0)) * (1.0 / 256)

    for out in outs:
        out.wait()
    left(s_snd.at[pl.ds(0, 7)], "spread")
    left(rows_a.at[0, pl.ds(0, 15)], "plane")
    left(rows_a.at[pl.ds(0, 3)], "ring")
    left(rows_a.at[pl.ds(0, 4)], "stud_side")
    left(gath.at[0, 0, pl.ds(0, 3), 0], "first")
    left(gath.at[0, pl.ds(0, 3), :, 0], "second")
    left(gath.at[pl.ds(0, 3), :, :, 0], "last")
    left(gath.at[:, :, :, 0], "side")
    left(st_rcv, "stats")
    left(ls_rcv.at[pl.ds(0, 10)], "loss")
    left(sib_snd, "sib")
    left(p1_snd.at[:, pl.ds(0, 3)], "line")
    left(p2_snd.at[:, pl.ds(0, 31)], "direct")
    for k, buf in enumerate((sl_snd, tl_snd, g_snd)):
        bulk_wait(buf, bulk_s, k)


def head_kernel(grad_hbm, rows_hbm, out_hbm, grad, rows, out, sems):
    load_grad = pltpu.make_async_copy(grad_hbm, grad, sems.at[16])
    load_grad.start()
    loads, stores = [], []
    for j in range(8):
        loads.append(pltpu.make_async_copy(rows_hbm.at[j], rows.at[j], sems.at[j]))
        loads[j].start()
    load_grad.wait()
    for j in range(8):
        cols = pl.ds(j * 512, 512)
        loads[j].wait()
        out[:, cols] = jnp.dot(
            grad[...], rows[j].reshape(256, 512), preferred_element_type=F32
        ).astype(BF16)
        stores.append(pltpu.make_async_copy(out.at[:, cols], out_hbm.at[:, cols], sems.at[8 + j]))
        stores[j].start()
    for store in stores:
        store.wait()


def body(
    teacher_hidden,
    teacher_gain,
    teacher_head,
    student_hidden,
    student_gain,
    student_head,
    token_ids,
    teacher_map,
    student_map,
):
    vmem = pl.BlockSpec(memory_space=pltpu.VMEM)
    hbm = pl.BlockSpec(memory_space=pltpu.HBM)
    loss, input_grad, grad, rows = pl.pallas_call(
        kernel,
        out_shape=(
            jax.ShapeDtypeStruct((1, 1), F32),
            jax.ShapeDtypeStruct((2, 4096), F32),
            jax.ShapeDtypeStruct((512, 256), BF16),
            jax.ShapeDtypeStruct((8, 16, 16, 512), BF16),
        ),
        in_specs=[hbm] * 9,
        out_specs=(pl.BlockSpec(memory_space=pltpu.SMEM), vmem, hbm, hbm),
        scratch_shapes=[
            pltpu.VMEM((4, 4, 4, 2, 128, 256), BF16),
            pltpu.VMEM((512, 16384), BF16),
            pltpu.VMEM((512, 4096), BF16),
            pltpu.VMEM((16384,), BF16),
            pltpu.VMEM((4096,), BF16),
            pltpu.VMEM((2, 4096), BF16),
            pltpu.VMEM((128,), jnp.int32),
            pltpu.VMEM((128,), jnp.int32),
            pltpu.VMEM((8, 128), jnp.int32),
            pltpu.SMEM((256,), jnp.int32),
            pltpu.SMEM((8, 128), jnp.int32),
            pltpu.VMEM((256, 512), F32),
            pltpu.VMEM((256, 512), F32),
            pltpu.VMEM((8, 16, 16, 512), BF16),
            pltpu.VMEM((8, 2, 512), BF16),
            pltpu.VMEM((8, 2, 512), BF16),
            pltpu.VMEM((5, 2, 8, 128), F32),
            pltpu.VMEM((10, 2, 8, 128), F32),
            pltpu.VMEM((2, 128, 128), F32),
            pltpu.VMEM((128, 8, 128), BF16),
            pltpu.VMEM((128, 8, 128), BF16),
            pltpu.VMEM((128, 8, 128), BF16),
            pltpu.VMEM((128, 8, 128), BF16),
            pltpu.VMEM((128, 8, 128), BF16),
            pltpu.VMEM((128, 8, 128), BF16),
            pltpu.VMEM((256, 512), BF16),
            pltpu.VMEM((512, 256), BF16),
            pltpu.VMEM((4, 4, 4, 16, 512), BF16),
            pltpu.VMEM((4, 4, 4, 16, 512), BF16),
            pltpu.VMEM((4, 4, 4, 16, 512), F32),
            pltpu.VMEM((4, 4, 4, 16, 512), BF16),
            pltpu.VMEM((4, 3, 4, 16, 512), BF16),
            pltpu.VMEM((2, 32, 2, 1024), BF16),
            pltpu.VMEM((2, 32, 2, 1024), BF16),
            pltpu.VMEM((5, 8, 128), F32),
            pltpu.VMEM((13, 8, 128), F32),
            pltpu.SemaphoreType.DMA((len(SEND),)),
            pltpu.SemaphoreType.DMA((N_RECV,)),
            pltpu.SemaphoreType.DMA((12,)),
            pltpu.SemaphoreType.DMA((3,)),
            pltpu.SemaphoreType.DMA((3,)),
        ],
        compiler_params=pltpu.CompilerParams(
            collective_id=0, has_side_effects=True, vmem_limit_bytes=63 << 20
        ),
        cost_estimate=pl.CostEstimate(
            flops=2 * 256 * 512 * (16384 + 3 * 4096), bytes_accessed=24 << 20, transcendentals=0
        ),
        name="distill",
    )(
        teacher_hidden,
        teacher_gain,
        teacher_head,
        student_hidden,
        student_gain,
        student_head,
        token_ids,
        teacher_map,
        student_map,
    )
    head_grad = pl.pallas_call(
        head_kernel,
        out_shape=jax.ShapeDtypeStruct((512, 4096), BF16),
        in_specs=[hbm, hbm],
        out_specs=hbm,
        scratch_shapes=[
            pltpu.VMEM((512, 256), BF16),
            pltpu.VMEM((8, 16, 16, 512), BF16),
            pltpu.VMEM((512, 4096), BF16),
            pltpu.SemaphoreType.DMA((17,)),
        ],
        compiler_params=pltpu.CompilerParams(vmem_limit_bytes=63 << 20),
        cost_estimate=pl.CostEstimate(
            flops=2 * 256 * 512 * 4096, bytes_accessed=6 << 20, transcendentals=0
        ),
        name="head",
    )(grad, rows)
    return (loss.reshape(()), head_grad, input_grad)


def solution(mesh):
    placed = (
        P("role", "vocab"),
        P(),
        P(("role", "vocab"), None),
        P(("role", "vocab"), None),
        P(),
        P(("role", "vocab"), None),
        P(),
        P(),
        P(),
    )
    return jax.shard_map(
        body,
        mesh=mesh,
        in_specs=placed,
        out_specs=(P(), P(("role", "vocab"), None), P(("role", "vocab"), None)),
        check_vma=False,
    )
```

```python
import jax
import jax.numpy as jnp
from jax import lax
from jax.experimental import pallas as pl
from jax.experimental.pallas import tpu as pltpu
from jax.sharding import PartitionSpec as P

EPS = 1e-05
LOSS_SCALE = 256.0
CE_WEIGHT = 0.25
MESH = pl.DeviceIdType.MESH
F32 = jnp.float32
BF16 = jnp.bfloat16
X, Y, Z = 0, 1, 2
ALL = pl.ds(0, 4)
PARTS = (((Y, Z, X), 0, 32), ((X, Z, Y), 32, 48), ((Y, X, Z), 80, 48))
SEND = {name: k for k, name in enumerate(
    ("spread", "plane", "ring", "stud_side", "first", "second", "last", "side", "stats", "loss", "sib", "line", "direct")
)}
RECV_COUNTS = dict(
    spread=1, plane=1, ring=4, far=1, stud_side=1, first=9, second=9, heavy=24, halves=12,
    side=2, stats=4, loss=4, sib=4, line=4, direct=2,
)
RECV = {name: sum(list(RECV_COUNTS.values())[:k]) for k, name in enumerate(RECV_COUNTS)}
N_RECV = sum(RECV_COUNTS.values())


def div(a, b):
    return lax.div(a, jnp.int32(b))


def rem(a, b):
    return lax.rem(a, jnp.int32(b))


def flat_of(x, y, z, c):
    return div(y, 2) * 64 + ((x * 2 + rem(y, 2)) * 4 + z) * 2 + c


def shuffle4(tiles, pair):
    out = []
    for b in range(4):
        acc = None
        for a in range(4):
            shift = (2 * (a - b)) % 8
            moved = pltpu.roll(tiles[a], shift, 0) if shift else tiles[a]
            acc = moved if acc is None else jnp.where(pair == a, moved, acc)
        out.append(acc)
    return out


def kernel(
    t_hbm,
    tg_hbm,
    th_hbm,
    s_hbm,
    sg_hbm,
    sh_hbm,
    ids_hbm,
    tm_hbm,
    sm_hbm,
    loss_ref,
    ig_ref,
    g2t_out,
    rows_out,
    gath,
    th,
    sh,
    tg,
    sg,
    s_ref,
    tmap,
    smap,
    order_vec,
    ids,
    order_ref,
    acc,
    acc_s,
    rows_a,
    s_snd,
    s_rcv,
    st_own,
    st_rcv,
    scale_ref,
    tl_snd,
    tl_rcv,
    sl_snd,
    sl_rcv,
    g_snd,
    g_rcv,
    g2_ref,
    g2t,
    sib_snd,
    sib_rcv,
    hb,
    p1_snd,
    p1_rcv,
    p2_snd,
    p2_rcv,
    ls_own,
    ls_rcv,
    ssem,
    rsem,
    lsem,
    bulk_s,
    bulk_r,
):
    role = lax.axis_index("role")
    vocab = lax.axis_index("vocab")
    me_c = rem(vocab, 2)
    me = (div(vocab, 16), role * 2 + rem(div(vocab, 8), 2), rem(div(vocab, 2), 4))
    flat = role * 64 + vocab
    j_me = me[X] * 2 + me_c
    g_me = me[Y] * 4 + me[Z]

    def device(x, y, z, c):
        return (div(y, 2), ((x * 2 + rem(y, 2)) * 4 + z) * 2 + c)

    def moved(axis, step):
        return rem(me[axis] + step, 4)

    def line(axis, step):
        at = list(me)
        at[axis] = moved(axis, step)
        return device(at[0], at[1], at[2], me_c)

    sibling = device(me[X], me[Y], me[Z], 1 - me_c)

    def column(k):
        return device(div(k, 2), me[Y], me[Z], rem(k, 2))

    def plane(dy, dz):
        return device(me[X], moved(Y, dy), moved(Z, dz), me_c)

    def send(src, dst, to, group, index=0, sender=None):
        pltpu.make_async_remote_copy(
            src,
            dst,
            ssem.at[SEND[sender or group]],
            rsem.at[RECV[group] + index],
            device_id=to,
            device_id_type=MESH,
        ).start()

    def arrived(ref, group, index=0):
        pltpu.make_async_copy(ref, ref, rsem.at[RECV[group] + index]).wait()

    def left(ref, sender):
        pltpu.make_async_copy(ref, ref, ssem.at[SEND[sender]]).wait()

    plane_steps = [(dy, dz) for dy in range(4) for dz in range(4) if (dy, dz) != (0, 0)]
    barrier = pltpu.get_barrier_semaphore()
    for k in range(1, 8):
        pl.semaphore_signal(barrier, inc=1, device_id=column(rem(j_me + k, 8)), device_id_type=MESH)
    for dy, dz in plane_steps:
        pl.semaphore_signal(barrier, inc=1, device_id=plane(dy, dz), device_id_type=MESH)

    own_slot = gath.at[me[X], me[Y], me[Z], me_c]
    loads = [
        pltpu.make_async_copy(src, dst, lsem.at[k])
        for k, (src, dst) in enumerate(
            (
                (t_hbm, own_slot),
                (s_hbm, s_ref),
                (sg_hbm, sg),
                (tg_hbm, tg),
                (tm_hbm, tmap),
                (sm_hbm, smap),
                (ids_hbm, ids),
                (sh_hbm, sh),
                (th_hbm, th),
            )
        )
    ]
    for load in loads[:7]:
        load.start()
    load_sh, load_th = loads[7:]

    loads[1].wait()
    loads[2].wait()
    stud = s_ref[...].astype(F32)
    stud_gain = sg[...].astype(F32).reshape(1, 4096)
    stud_scale = lax.rsqrt(jnp.mean(stud * stud, axis=1, keepdims=True) + EPS)
    stud_normed = (stud * stud_scale * stud_gain).astype(BF16)
    for j in range(8):
        s_snd[j] = stud_normed[:, j * 512 : (j + 1) * 512]
    s_rcv[j_me] = s_snd[j_me]
    loads[0].wait()
    own_f = own_slot[...].astype(F32)
    sums = jnp.sum(own_f * own_f, axis=1, keepdims=True)
    flipped = jnp.broadcast_to(sums, (128, 128)).T[:8]
    st_own[0, 0] = jnp.where(role == 0, flipped, 0.0)
    st_own[0, 1] = jnp.where(role == 1, flipped, 0.0)

    pl.semaphore_wait(barrier, 22)

    def at(part, a, b, c):
        (first, second, last), start, count = PARTS[part]
        index = [None, None, None]
        index[first], index[second], index[last] = a, b, c
        return gath.at[index[0], index[1], index[2], me_c, pl.ds(start, count)]

    def axes(part):
        return PARTS[part][0]

    parts = range(3)
    steps = (1, 3, 2)

    for k in range(1, 8):
        to = rem(j_me + k, 8)
        send(s_snd.at[to], s_rcv.at[j_me], column(to), "spread")

    def no(p, d):
        return p * 3 + steps.index(d)

    def last_no(p, g, d):
        return (p * 4 + g) * 2 + d // 2

    def mine(p):
        a, b, c = axes(p)
        return at(p, me[a], me[b], me[c])

    for p in parts:
        a, b, c = axes(p)
        for d in steps:
            send(mine(p), mine(p), line(a, d), "first", no(p, d))
    for p in parts:
        a, b, c = axes(p)
        for d in (1, 3):
            send(mine(p), mine(p), line(c, d), "heavy", last_no(p, 0, d), "last")
        for d in steps:
            send(mine(p), mine(p), line(b, d), "second", no(p, d))
    def spread_stats(stage):
        for i, d in enumerate(steps):
            send(st_own.at[stage], st_rcv.at[stage * 3 + i], line((X, Y, Z)[stage], d), "stats", stage)

    def add_stats(stage):
        arrived(st_rcv.at[pl.ds(stage * 3, 3)], "stats", stage)
        total = st_own[stage]
        for i in range(3):
            total = total + st_rcv[stage * 3 + i]
        st_own[stage + 1] = total

    spread_stats(0)

    def to_side(g, ref):
        send(ref, ref, sibling, "side", g // 3)

    def to_stud_side(ref):
        send(ref, ref, sibling, "stud_side")

    def offset_b(p, g):
        return moved(axes(p)[1], (0, 3, 1, 2)[g])

    arrived(s_rcv.at[pl.ds(0, 7)], "spread")
    tile = jnp.concatenate([s_rcv[k].astype(F32) for k in range(8)], axis=0)
    rows_a[j_me, g_me] = tile.astype(BF16)
    tile_ref = rows_a.at[j_me, g_me]
    for dy, dz in plane_steps:
        send(tile_ref, tile_ref, plane(dy, dz), "plane")

    for d in steps:
        for p in parts:
            a, b, c = axes(p)
            block = at(p, moved(a, 4 - d), me[b], me[c])
            arrived(block, "first", no(p, d))
            for e in steps:
                send(block, block, line(b, e), "second", no(p, e))
            for e in (1, 3):
                send(block, block, line(c, e), "heavy", last_no(p, 0, e), "last")
    for p in parts:
        a, b, c = axes(p)
        to_side(0, at(p, ALL, me[b], me[c]))

    low, high = pl.ds(0, 8), pl.ds(8, 8)
    ways = ((1, low, 0), (3, high, 1), (1, high, 2), (3, low, 3))

    def chunk(step, half=pl.ds(0, 16)):
        return rows_a.at[moved(X, step) * 2 + me_c, half]

    arrived(rows_a.at[j_me, pl.ds(0, 15)], "plane")
    for d, half, n in ways:
        send(chunk(0, half), chunk(0, half), line(X, d), "ring", n)
    to_stud_side(chunk(0))
    add_stats(0)
    spread_stats(1)

    for g, d in enumerate(steps):
        for p in parts:
            a, b, c = axes(p)
            group = at(p, ALL, offset_b(p, g + 1), me[c])
            arrived(group, "second", no(p, d))
            for e in (1, 3):
                send(group, group, line(c, e), "heavy", last_no(p, g + 1, e), "last")
            to_side(g + 1, group)
    for load in loads[7:]:
        load.start()

    for load in loads[3:7]:
        load.wait()
    held = jnp.broadcast_to(tmap[...].astype(F32).reshape(1, 128), (128, 128)).T
    student_map = smap[...].astype(F32).reshape(1, 128)
    down = lax.broadcasted_iota(jnp.int32, (128, 128), 0).astype(F32)
    found = jnp.max(jnp.where(held == student_map, down, 0.0), axis=0, keepdims=True)
    order_vec[...] = jnp.broadcast_to(found, (8, 128)).astype(jnp.int32)
    load_order = pltpu.make_async_copy(order_vec, order_ref, lsem.at[9])
    load_order.start()

    two = ((1, pl.ds(0, 2)), (3, pl.ds(2, 2)))

    def pass_heavy(g, which=parts):
        for p in which:
            c = axes(p)[2]
            for d, half in two:
                from_c = moved(c, 4 - d)
                group = at(p, ALL, offset_b(p, g), from_c)
                arrived(group, "heavy", last_no(p, g, d))
                piece = at(p, half, offset_b(p, g), from_c)
                send(piece, piece, line(c, d), "halves", p * 4 + g, "last")
                to_side(g, group)

    def pass_halves(g):
        for p in parts:
            c = axes(p)[2]
            group = at(p, ALL, offset_b(p, g), moved(c, 2))
            arrived(group, "halves", p * 4 + g)
            to_side(g, group)

    pass_heavy(0)
    add_stats(1)
    spread_stats(2)
    for d, half, n in ways[:2]:
        piece = chunk(4 - d, half)
        arrived(piece, "ring", n)
        send(piece, piece, line(X, d), "far", 0, "ring")
        to_stud_side(piece)
    pass_heavy(1)
    for d, half, n in ways[2:]:
        piece = chunk(4 - d, half)
        arrived(piece, "ring", n)
        to_stud_side(piece)
    pass_halves(0)
    arrived(chunk(2), "far")
    to_stud_side(chunk(2))
    add_stats(2)
    send(st_own.at[3], st_rcv.at[9], sibling, "stats", 3)
    pass_heavy(2)
    pass_halves(1)

    sub = lax.broadcasted_iota(jnp.int32, (8, 128), 0)
    lane = lax.broadcasted_iota(jnp.int32, (8, 128), 1)
    pair = sub // 2

    def fill_messages(source, which, r, index):
        rows = source[pl.ds(pl.multiple_of(r * 8, 8), 8), :]
        tiles = shuffle4([rows[:, j * 128 : (j + 1) * 128] for j in range(4)], pair)
        for k in range(4):
            which[index(r, jnp.int32(k))] = tiles[k].astype(BF16)

    role_at = [div(moved(Y, b), 2) for b in range(4)]
    y_at = [rem(moved(Y, b), 2) * 8 for b in range(4)]
    x_at = [moved(X, a) * 16 for a in range(4)]
    z_at = [moved(Z, c) * 2 for c in range(4)]
    c_at = [me_c, 1 - me_c]
    near_last = sorted(
        ((a, c, e) for a in range(4) for c in range(4) for e in range(2)),
        key=lambda place: (-min(place[0], 4 - place[0]) - min(place[1], 4 - place[1]), -place[2]),
    )

    def send_plane(snd, rcv, sem, b):
        for a, c, e in near_last:
            if (a, b, c, e) != (0, 0, 0, 0):
                vocab_to = x_at[a] + y_at[b] + z_at[c] + c_at[e]
                pltpu.make_async_remote_copy(
                    snd.at[role_at[b] * 64 + vocab_to],
                    rcv.at[flat],
                    bulk_s.at[sem],
                    bulk_r.at[sem],
                    device_id=(role_at[b], vocab_to),
                    device_id_type=MESH,
                ).start()

    planes = (2, 1, 3, 0)

    def column_index(r, k):
        g = div(r, 2)
        return flat_of(rem(r, 2) * 2 + div(k, 2), div(g, 4), rem(g, 4), rem(k, 2))

    def plain_index(r, k):
        return r * 4 + k

    def bulk_wait(buf, sems, sem):
        pltpu.make_async_copy(buf.at[pl.ds(0, 127)], buf.at[pl.ds(0, 127)], sems.at[sem]).wait()

    arrived(rows_a.at[pl.ds(0, 4)], "stud_side")
    load_sh.wait()
    for j in range(8):
        part = lax.dot_general(
            rows_a[j].reshape(256, 512),
            sh[:, j * 512 : (j + 1) * 512],
            (((1,), (1,)), ((), ())),
            preferred_element_type=F32,
        )
        if j == 0:
            acc_s[...] = part
        else:
            acc_s[...] += part

    @pl.loop(0, 32, unroll=4)
    def _(r):
        fill_messages(acc_s, sl_snd, r, column_index)

    sl_rcv[flat] = sl_snd[flat]

    for p in parts:
        send_plane(sl_snd, sl_rcv, 0, planes[p])
        pass_heavy(3, (p,))
    send_plane(sl_snd, sl_rcv, 0, 0)
    pass_halves(2)
    outs = [pltpu.make_async_copy(rows_a, rows_out, lsem.at[10])]
    outs[0].start()
    arrived(st_rcv.at[9], "stats", 3)
    for r in range(2):
        total = st_own[3, r] + st_rcv[9, r]
        scale = lax.rsqrt(total * (1.0 / 16384) + EPS)
        scale_ref[r] = jnp.broadcast_to(scale[0:1], (128, 128)).T

    load_th.wait()
    arrived(gath.at[pl.ds(0, 3), :, :, 0], "side", 0)
    acc[...] = jnp.zeros_like(acc)

    def teacher_step(dx, dz):
        x, z = rem(me[X] + dx, 4), rem(me[Z] + dz, 4)
        lanes, heads = [], []
        for y_lo in range(2):
            base = pl.multiple_of(x * 4096 + y_lo * 2048 + z * 512, 512)
            gain = tg[pl.ds(base, 512)].astype(F32).reshape(1, 512)
            heads.append(th[:, pl.ds(base, 512)])
            for c in range(2):
                rows = []
                for r in range(2):
                    block = gath[x, 2 * r + y_lo, z, c].astype(F32)
                    scale = scale_ref[r]
                    scale = jnp.concatenate([scale, scale], axis=1)
                    rows.append((block * scale * gain[:, c * 256 : (c + 1) * 256]).astype(BF16))
                lanes.append(jnp.concatenate(rows, axis=0))
        acc[...] += lax.dot_general(
            jnp.concatenate(lanes, axis=1),
            jnp.concatenate(heads, axis=1),
            (((1,), (1,)), ((), ())),
            preferred_element_type=F32,
        )

    @pl.loop(0, 9)
    def _(i):
        q, w = div(i, 3), rem(i, 3)
        teacher_step(q + div(q, 2), w + div(w, 2))

    pass_halves(3)

    arrived(gath.at[0, :, :, 0], "side", 1)

    @pl.loop(0, 4)
    def _(i):
        teacher_step(2, i)

    @pl.loop(0, 3)
    def _(q):
        teacher_step(q + div(q, 2), 2)

    for b in planes:
        base = role_at[b] * 16 + div(y_at[b], 4)

        @pl.loop(0, 8, unroll=4)
        def _(i, base=base):
            fill_messages(acc, tl_snd, base + i + 2 * div(i, 2), plain_index)

        send_plane(tl_snd, tl_rcv, 1, b)
    tl_rcv[flat] = tl_snd[flat]

    def over(value, op, reduce):
        value = jnp.broadcast_to(reduce(value, axis=1, keepdims=True), (8, 128))
        value = op(value, pltpu.roll(value, 2, 0))
        return op(value, pltpu.roll(value, 4, 0))

    def log_sum(ref):
        def top_step(i, top):
            return jnp.maximum(top, jnp.max(ref[pl.ds(i * 16, 16)].astype(F32), axis=0))

        top = lax.fori_loop(0, 8, top_step, jnp.full((8, 128), -jnp.inf, F32))
        top = over(top, jnp.maximum, jnp.max)

        def sum_step(i, total):
            part = jnp.exp(ref[pl.ds(i * 16, 16)].astype(F32) - top[None])
            return total + jnp.sum(part, axis=0)

        total = lax.fori_loop(0, 8, sum_step, jnp.zeros((8, 128), F32))
        return top + jnp.log(over(total, jnp.add, jnp.sum))

    load_order.wait()
    bulk_wait(sl_rcv, bulk_r, 0)
    stud_log = log_sum(sl_rcv)
    bulk_wait(tl_rcv, bulk_r, 1)
    teach_log = log_sum(tl_rcv)
    token = sub % 2
    lane_row = lax.broadcasted_iota(jnp.int32, (1, 128), 1).astype(F32)

    def label_place(label):
        block = div(label, 512)
        match = smap[...].astype(F32).reshape(1, 128) == block.astype(F32)
        place = jnp.sum(jnp.where(match, lane_row, 0.0), axis=1, keepdims=True)
        return place.astype(jnp.int32) * 512 + (label - block * 512)

    wanted = jnp.where(token == 0, label_place(ids[flat * 2]), label_place(ids[flat * 2 + 1]))
    place = pair * 128 + lane

    def term(i, carry):
        teach = tl_rcv[jnp.clip(order_ref[0, i], 0, 127)].astype(F32)
        student = sl_rcv[i].astype(F32)
        teach_prob = jnp.exp(teach - teach_log)
        stud_prob = jnp.exp(student - stud_log)
        hit = (place + i * 512) == wanted
        grad = LOSS_SCALE * (
            (1.0 + CE_WEIGHT) * stud_prob - teach_prob - CE_WEIGHT * hit.astype(F32)
        )
        g_snd[i] = grad.astype(BF16)
        return carry + teach_prob * (teach - student) - CE_WEIGHT * jnp.where(hit, student, 0.0)

    total = jnp.zeros((8, 128), F32)
    for b in planes:
        base = role_at[b] * 64 + y_at[b]
        total = lax.fori_loop(
            0, 32, lambda j, carry, base=base: term(base + j + 8 * div(j, 8), carry), total, unroll=8
        )
        send_plane(g_snd, g_rcv, 2, b)
    g_rcv[flat] = g_snd[flat]
    once = (sub < 2) & (lane == 0)
    total = total + jnp.where(once, (1.0 + CE_WEIGHT) * stud_log - teach_log, 0.0)
    total = jnp.sum(jnp.sum(total, axis=1, keepdims=True), axis=0, keepdims=True)
    ls_own[0] = jnp.broadcast_to(total, (8, 128))
    send(ls_own.at[0], ls_rcv.at[0], sibling, "loss", 0)

    def add_loss(stage):
        base = 4 * stage - 3
        axis = (Y, Z, X)[stage - 1]
        arrived(ls_rcv.at[pl.ds(base, 3)], "loss", stage)
        total = jnp.zeros((8, 128), F32)
        for i in range(4):
            total = total + jnp.where(me[axis] == i, ls_own[stage], ls_rcv[base + i])
        ls_own[stage + 1] = total

    def spread_loss(stage):
        base = 4 * stage - 3
        axis = (Y, Z, X)[stage - 1]
        for d in steps:
            send(ls_own.at[stage], ls_rcv.at[base + me[axis]], line(axis, d), "loss", stage)

    for i in range(3):
        ls_rcv[1 + 4 * i + me[(Y, Z, X)[i]]] = jnp.zeros((8, 128), F32)
    arrived(ls_rcv.at[0], "loss", 0)
    ls_own[1] = ls_own[0] + ls_rcv[0]
    spread_loss(1)

    bulk_wait(g_rcv, bulk_r, 2)

    @pl.loop(0, 16)
    def _(g):
        rows = []
        for h in range(2):
            msgs = [g_rcv[column_index(g * 2 + h, k)].astype(F32) for k in range(4)]
            rows.append(jnp.concatenate(shuffle4(msgs, pair), axis=1))
        start = pl.multiple_of(g * 16, 16)
        g2_ref[pl.ds(start, 16), :] = jnp.concatenate(rows, axis=0).astype(BF16)

    def hidden_cols(core, part):
        cols = pl.ds(pl.multiple_of(core * 2048 + part * 512, 512), 512)
        value = jnp.dot(g2_ref[...], sh[:, cols], preferred_element_type=F32)
        return value.reshape(4, 4, 16, 512)

    for part in range(4):
        sib_snd[part] = hidden_cols(1 - me_c, part).astype(BF16)
        send(sib_snd.at[part], sib_rcv.at[part], sibling, "sib", part)
    for part in range(4):
        hb[part] = hidden_cols(me_c, part)
    add_loss(1)
    spread_loss(2)

    for part in range(4):
        axis = (Y, Z)[part % 2]
        arrived(sib_rcv.at[part], "sib", part)
        summed = hb[part] + sib_rcv[part].astype(F32)
        hb[part] = summed
        p1_snd[part] = (summed if axis == Y else jnp.swapaxes(summed, 0, 1)).astype(BF16)
        for i, d in enumerate(steps):
            send(p1_snd.at[part, moved(axis, d)], p1_rcv.at[part, i], line(axis, d), "line", part)

    g2t[...] = g2_ref[...].astype(F32).T.astype(BF16)
    outs.append(pltpu.make_async_copy(g2t, g2t_out, lsem.at[11]))
    outs[1].start()
    add_loss(2)
    spread_loss(3)

    for way, axis in enumerate((Y, Z)):
        for h in range(2):
            part = way + 2 * h
            total = hb[part, me[Y]] if axis == Y else hb[part, :, me[Z]]
            arrived(p1_rcv.at[part], "line", part)
            for i in range(3):
                total = total + p1_rcv[part, i].astype(F32)
            for q in range(4):
                for k in range(8):
                    p2_snd[way, q * 8 + k, :, h * 512 : (h + 1) * 512] = total[q, 2 * k : 2 * k + 2].astype(BF16)
        own = (me[Z] if axis == Y else me[Y]) * 8 + j_me
        p2_rcv[way, own] = p2_snd[way, own]
        other = Z if axis == Y else Y
        for a, o, e in near_last:
            if (a, o, e) == (0, 0, 0):
                continue
            q, x, c = moved(other, o), moved(X, a), c_at[e]
            to = q * 8 + x * 2 + c
            y, z = (me[Y], q) if axis == Y else (q, me[Z])
            send(
                p2_snd.at[way, to], p2_rcv.at[way, own], device(x, y, z, c), "direct", way
            )
    for way in range(2):
        arrived(p2_rcv.at[way, pl.ds(0, 31)], "direct", way)
    back = []
    for c in range(2):
        sums = []
        for way in range(2):
            total = jnp.zeros((2, 1024), F32)
            for k in range(16):
                total = total + p2_rcv[way, k * 2 + c].astype(F32)
            sums.append(total)
        for part in range(4):
            back.append(sums[part % 2][:, part // 2 * 512 : (part // 2 + 1) * 512])
    back = jnp.concatenate(back, axis=1) * sg[...].astype(F32).reshape(1, 4096)
    hat = s_ref[...].astype(F32) * stud_scale
    ig_ref[...] = stud_scale * (back - hat * jnp.mean(back * hat, axis=1, keepdims=True))
    add_loss(3)
    loss_ref[0, 0] = jnp.sum(jnp.where((sub == 0) & (lane == 0), ls_own[4], 0.0)) * (1.0 / 256)

    for out in outs:
        out.wait()
    left(s_snd.at[pl.ds(0, 7)], "spread")
    left(rows_a.at[0, pl.ds(0, 15)], "plane")
    left(rows_a.at[pl.ds(0, 3)], "ring")
    left(rows_a.at[pl.ds(0, 4)], "stud_side")
    left(gath.at[0, 0, pl.ds(0, 3), 0], "first")
    left(gath.at[0, pl.ds(0, 3), :, 0], "second")
    left(gath.at[pl.ds(0, 3), :, :, 0], "last")
    left(gath.at[:, :, :, 0], "side")
    left(st_rcv, "stats")
    left(ls_rcv.at[pl.ds(0, 10)], "loss")
    left(sib_snd, "sib")
    left(p1_snd.at[:, pl.ds(0, 3)], "line")
    left(p2_snd.at[:, pl.ds(0, 31)], "direct")
    for k, buf in enumerate((sl_snd, tl_snd, g_snd)):
        bulk_wait(buf, bulk_s, k)


def head_kernel(grad_hbm, rows_hbm, ig_hbm, out_hbm, ig_out, grad, rows, out, sems):
    move_ig = pltpu.make_async_copy(ig_hbm, ig_out, sems.at[17])
    move_ig.start()
    load_grad = pltpu.make_async_copy(grad_hbm, grad, sems.at[16])
    load_grad.start()
    loads, stores = [], []
    for j in range(8):
        loads.append(pltpu.make_async_copy(rows_hbm.at[j], rows.at[j], sems.at[j]))
        loads[j].start()
    load_grad.wait()
    for j in range(8):
        cols = pl.ds(j * 512, 512)
        loads[j].wait()
        out[:, cols] = jnp.dot(
            grad[...], rows[j].reshape(256, 512), preferred_element_type=F32
        ).astype(BF16)
        stores.append(pltpu.make_async_copy(out.at[:, cols], out_hbm.at[:, cols], sems.at[8 + j]))
        stores[j].start()
    for store in stores:
        store.wait()
    move_ig.wait()


def body(
    teacher_hidden,
    teacher_gain,
    teacher_head,
    student_hidden,
    student_gain,
    student_head,
    token_ids,
    teacher_map,
    student_map,
):
    vmem = pl.BlockSpec(memory_space=pltpu.VMEM)
    hbm = pl.BlockSpec(memory_space=pltpu.HBM)
    loss, input_grad, grad, rows = pl.pallas_call(
        kernel,
        out_shape=(
            jax.ShapeDtypeStruct((1, 1), F32),
            jax.ShapeDtypeStruct((2, 4096), F32),
            jax.ShapeDtypeStruct((512, 256), BF16),
            jax.ShapeDtypeStruct((8, 16, 16, 512), BF16),
        ),
        in_specs=[hbm] * 9,
        out_specs=(pl.BlockSpec(memory_space=pltpu.SMEM), vmem, hbm, hbm),
        scratch_shapes=[
            pltpu.VMEM((4, 4, 4, 2, 128, 256), BF16),
            pltpu.VMEM((512, 16384), BF16),
            pltpu.VMEM((512, 4096), BF16),
            pltpu.VMEM((16384,), BF16),
            pltpu.VMEM((4096,), BF16),
            pltpu.VMEM((2, 4096), BF16),
            pltpu.VMEM((128,), jnp.int32),
            pltpu.VMEM((128,), jnp.int32),
            pltpu.VMEM((8, 128), jnp.int32),
            pltpu.SMEM((256,), jnp.int32),
            pltpu.SMEM((8, 128), jnp.int32),
            pltpu.VMEM((256, 512), F32),
            pltpu.VMEM((256, 512), F32),
            pltpu.VMEM((8, 16, 16, 512), BF16),
            pltpu.VMEM((8, 2, 512), BF16),
            pltpu.VMEM((8, 2, 512), BF16),
            pltpu.VMEM((5, 2, 8, 128), F32),
            pltpu.VMEM((10, 2, 8, 128), F32),
            pltpu.VMEM((2, 128, 128), F32),
            pltpu.VMEM((128, 8, 128), BF16),
            pltpu.VMEM((128, 8, 128), BF16),
            pltpu.VMEM((128, 8, 128), BF16),
            pltpu.VMEM((128, 8, 128), BF16),
            pltpu.VMEM((128, 8, 128), BF16),
            pltpu.VMEM((128, 8, 128), BF16),
            pltpu.VMEM((256, 512), BF16),
            pltpu.VMEM((512, 256), BF16),
            pltpu.VMEM((4, 4, 4, 16, 512), BF16),
            pltpu.VMEM((4, 4, 4, 16, 512), BF16),
            pltpu.VMEM((4, 4, 4, 16, 512), F32),
            pltpu.VMEM((4, 4, 4, 16, 512), BF16),
            pltpu.VMEM((4, 3, 4, 16, 512), BF16),
            pltpu.VMEM((2, 32, 2, 1024), BF16),
            pltpu.VMEM((2, 32, 2, 1024), BF16),
            pltpu.VMEM((5, 8, 128), F32),
            pltpu.VMEM((13, 8, 128), F32),
            pltpu.SemaphoreType.DMA((len(SEND),)),
            pltpu.SemaphoreType.DMA((N_RECV,)),
            pltpu.SemaphoreType.DMA((12,)),
            pltpu.SemaphoreType.DMA((3,)),
            pltpu.SemaphoreType.DMA((3,)),
        ],
        compiler_params=pltpu.CompilerParams(
            collective_id=0, has_side_effects=True, vmem_limit_bytes=63 << 20
        ),
        cost_estimate=pl.CostEstimate(
            flops=2 * 256 * 512 * (16384 + 3 * 4096), bytes_accessed=24 << 20, transcendentals=0
        ),
        name="distill",
    )(
        teacher_hidden,
        teacher_gain,
        teacher_head,
        student_hidden,
        student_gain,
        student_head,
        token_ids,
        teacher_map,
        student_map,
    )
    head_grad, input_grad = pl.pallas_call(
        head_kernel,
        out_shape=(
            jax.ShapeDtypeStruct((512, 4096), BF16),
            jax.ShapeDtypeStruct((2, 4096), F32),
        ),
        in_specs=[hbm, hbm, hbm],
        out_specs=(hbm, hbm),
        scratch_shapes=[
            pltpu.VMEM((512, 256), BF16),
            pltpu.VMEM((8, 16, 16, 512), BF16),
            pltpu.VMEM((512, 4096), BF16),
            pltpu.SemaphoreType.DMA((18,)),
        ],
        compiler_params=pltpu.CompilerParams(vmem_limit_bytes=63 << 20),
        cost_estimate=pl.CostEstimate(
            flops=2 * 256 * 512 * 4096, bytes_accessed=6 << 20, transcendentals=0
        ),
        name="head",
    )(grad, rows, input_grad)
    return (loss.reshape(()), head_grad, input_grad)


def solution(mesh):
    placed = (
        P("role", "vocab"),
        P(),
        P(("role", "vocab"), None),
        P(("role", "vocab"), None),
        P(),
        P(("role", "vocab"), None),
        P(),
        P(),
        P(),
    )
    return jax.shard_map(
        body,
        mesh=mesh,
        in_specs=placed,
        out_specs=(P(), P(("role", "vocab"), None), P(("role", "vocab"), None)),
        check_vma=False,
    )
```

```python
import jax
import jax.numpy as jnp
from jax import lax
from jax.experimental import pallas as pl
from jax.experimental.pallas import tpu as pltpu
from jax.sharding import PartitionSpec as P

EPS = 1e-05
LOSS_SCALE = 256.0
CE_WEIGHT = 0.25
MESH = pl.DeviceIdType.MESH
F32 = jnp.float32
BF16 = jnp.bfloat16
X, Y, Z = 0, 1, 2
ALL = pl.ds(0, 4)
PARTS = (((Y, Z, X), 0, 32), ((X, Z, Y), 32, 48), ((Y, X, Z), 80, 48))
SEND = {name: k for k, name in enumerate(
    ("spread", "plane", "ring", "stud_side", "first", "second", "last", "side", "stats", "loss", "sib", "line", "direct")
)}
RECV_COUNTS = dict(
    spread=1, plane=1, ring=4, far=1, stud_side=1, first=9, second=9, heavy=24, halves=12,
    side=3, stats=4, loss=4, sib=4, line=4, direct=2,
)
RECV = {name: sum(list(RECV_COUNTS.values())[:k]) for k, name in enumerate(RECV_COUNTS)}
N_RECV = sum(RECV_COUNTS.values())


def div(a, b):
    return lax.div(a, jnp.int32(b))


def rem(a, b):
    return lax.rem(a, jnp.int32(b))


def flat_of(x, y, z, c):
    return div(y, 2) * 64 + ((x * 2 + rem(y, 2)) * 4 + z) * 2 + c


def shuffle4(tiles, pair):
    out = []
    for b in range(4):
        acc = None
        for a in range(4):
            shift = (2 * (a - b)) % 8
            moved = pltpu.roll(tiles[a], shift, 0) if shift else tiles[a]
            acc = moved if acc is None else jnp.where(pair == a, moved, acc)
        out.append(acc)
    return out


def kernel(
    t_hbm,
    tg_hbm,
    th_hbm,
    s_hbm,
    sg_hbm,
    sh_hbm,
    ids_hbm,
    tm_hbm,
    sm_hbm,
    loss_ref,
    ig_ref,
    g2t_out,
    rows_out,
    gath,
    th,
    sh,
    tg,
    sg,
    s_ref,
    tmap,
    smap,
    order_vec,
    ids,
    order_ref,
    acc,
    acc_s,
    rows_a,
    s_snd,
    s_rcv,
    st_own,
    st_rcv,
    scale_ref,
    tl_snd,
    tl_rcv,
    sl_snd,
    sl_rcv,
    g_snd,
    g_rcv,
    g2_ref,
    g2t,
    sib_snd,
    sib_rcv,
    hb,
    p1_snd,
    p1_rcv,
    p2_snd,
    p2_rcv,
    ls_own,
    ls_rcv,
    ssem,
    rsem,
    lsem,
    bulk_s,
    bulk_r,
):
    role = lax.axis_index("role")
    vocab = lax.axis_index("vocab")
    me_c = rem(vocab, 2)
    me = (div(vocab, 16), role * 2 + rem(div(vocab, 8), 2), rem(div(vocab, 2), 4))
    flat = role * 64 + vocab
    j_me = me[X] * 2 + me_c
    g_me = me[Y] * 4 + me[Z]

    def device(x, y, z, c):
        return (div(y, 2), ((x * 2 + rem(y, 2)) * 4 + z) * 2 + c)

    def moved(axis, step):
        return rem(me[axis] + step, 4)

    def line(axis, step):
        at = list(me)
        at[axis] = moved(axis, step)
        return device(at[0], at[1], at[2], me_c)

    sibling = device(me[X], me[Y], me[Z], 1 - me_c)

    def column(k):
        return device(div(k, 2), me[Y], me[Z], rem(k, 2))

    def plane(dy, dz):
        return device(me[X], moved(Y, dy), moved(Z, dz), me_c)

    def send(src, dst, to, group, index=0, sender=None):
        pltpu.make_async_remote_copy(
            src,
            dst,
            ssem.at[SEND[sender or group]],
            rsem.at[RECV[group] + index],
            device_id=to,
            device_id_type=MESH,
        ).start()

    def arrived(ref, group, index=0):
        pltpu.make_async_copy(ref, ref, rsem.at[RECV[group] + index]).wait()

    def left(ref, sender):
        pltpu.make_async_copy(ref, ref, ssem.at[SEND[sender]]).wait()

    plane_steps = [(dy, dz) for dy in range(4) for dz in range(4) if (dy, dz) != (0, 0)]
    barrier = pltpu.get_barrier_semaphore()
    for k in range(1, 8):
        pl.semaphore_signal(barrier, inc=1, device_id=column(rem(j_me + k, 8)), device_id_type=MESH)
    for dy, dz in plane_steps:
        pl.semaphore_signal(barrier, inc=1, device_id=plane(dy, dz), device_id_type=MESH)

    own_slot = gath.at[me[X], me[Y], me[Z], me_c]
    loads = [
        pltpu.make_async_copy(src, dst, lsem.at[k])
        for k, (src, dst) in enumerate(
            (
                (t_hbm, own_slot),
                (s_hbm, s_ref),
                (sg_hbm, sg),
                (tg_hbm, tg),
                (tm_hbm, tmap),
                (sm_hbm, smap),
                (ids_hbm, ids),
                (sh_hbm, sh),
                (th_hbm, th),
            )
        )
    ]
    for load in loads[:7]:
        load.start()
    load_sh, load_th = loads[7:]

    loads[1].wait()
    loads[2].wait()
    stud = s_ref[...].astype(F32)
    stud_gain = sg[...].astype(F32).reshape(1, 4096)
    stud_scale = lax.rsqrt(jnp.mean(stud * stud, axis=1, keepdims=True) + EPS)
    stud_normed = (stud * stud_scale * stud_gain).astype(BF16)
    for j in range(8):
        s_snd[j] = stud_normed[:, j * 512 : (j + 1) * 512]
    s_rcv[j_me] = s_snd[j_me]
    loads[0].wait()
    own_f = own_slot[...].astype(F32)
    sums = jnp.sum(own_f * own_f, axis=1, keepdims=True)
    flipped = jnp.broadcast_to(sums, (128, 128)).T[:8]
    st_own[0, 0] = jnp.where(role == 0, flipped, 0.0)
    st_own[0, 1] = jnp.where(role == 1, flipped, 0.0)

    pl.semaphore_wait(barrier, 22)

    def at(part, a, b, c):
        (first, second, last), start, count = PARTS[part]
        index = [None, None, None]
        index[first], index[second], index[last] = a, b, c
        return gath.at[index[0], index[1], index[2], me_c, pl.ds(start, count)]

    def axes(part):
        return PARTS[part][0]

    parts = range(3)
    steps = (1, 3, 2)

    for k in range(1, 8):
        to = rem(j_me + k, 8)
        send(s_snd.at[to], s_rcv.at[j_me], column(to), "spread")

    def no(p, d):
        return p * 3 + steps.index(d)

    def last_no(p, g, d):
        return (p * 4 + g) * 2 + d // 2

    def mine(p):
        a, b, c = axes(p)
        return at(p, me[a], me[b], me[c])

    for p in parts:
        a, b, c = axes(p)
        for d in steps:
            send(mine(p), mine(p), line(a, d), "first", no(p, d))
    for p in parts:
        a, b, c = axes(p)
        for d in (1, 3):
            send(mine(p), mine(p), line(c, d), "heavy", last_no(p, 0, d), "last")
        for d in steps:
            send(mine(p), mine(p), line(b, d), "second", no(p, d))
    def spread_stats(stage):
        for i, d in enumerate(steps):
            send(st_own.at[stage], st_rcv.at[stage * 3 + i], line((X, Y, Z)[stage], d), "stats", stage)

    def add_stats(stage):
        arrived(st_rcv.at[pl.ds(stage * 3, 3)], "stats", stage)
        total = st_own[stage]
        for i in range(3):
            total = total + st_rcv[stage * 3 + i]
        st_own[stage + 1] = total

    spread_stats(0)

    def to_side(g, ref):
        send(ref, ref, sibling, "side", max(g - 1, 0))

    def to_stud_side(ref):
        send(ref, ref, sibling, "stud_side")

    def offset_b(p, g):
        return moved(axes(p)[1], (0, 3, 1, 2)[g])

    arrived(s_rcv.at[pl.ds(0, 7)], "spread")
    tile = jnp.concatenate([s_rcv[k].astype(F32) for k in range(8)], axis=0)
    rows_a[j_me, g_me] = tile.astype(BF16)
    tile_ref = rows_a.at[j_me, g_me]
    for dy, dz in plane_steps:
        send(tile_ref, tile_ref, plane(dy, dz), "plane")

    for d in steps:
        for p in parts:
            a, b, c = axes(p)
            block = at(p, moved(a, 4 - d), me[b], me[c])
            arrived(block, "first", no(p, d))
            for e in steps:
                send(block, block, line(b, e), "second", no(p, e))
            for e in (1, 3):
                send(block, block, line(c, e), "heavy", last_no(p, 0, e), "last")
    for p in parts:
        a, b, c = axes(p)
        to_side(0, at(p, ALL, me[b], me[c]))

    low, high = pl.ds(0, 8), pl.ds(8, 8)
    ways = ((1, low, 0), (3, high, 1), (1, high, 2), (3, low, 3))

    def chunk(step, half=pl.ds(0, 16)):
        return rows_a.at[moved(X, step) * 2 + me_c, half]

    arrived(rows_a.at[j_me, pl.ds(0, 15)], "plane")
    for d, half, n in ways:
        send(chunk(0, half), chunk(0, half), line(X, d), "ring", n)
    to_stud_side(chunk(0))
    add_stats(0)
    spread_stats(1)

    for g, d in enumerate(steps):
        for p in parts:
            a, b, c = axes(p)
            group = at(p, ALL, offset_b(p, g + 1), me[c])
            arrived(group, "second", no(p, d))
            for e in (1, 3):
                send(group, group, line(c, e), "heavy", last_no(p, g + 1, e), "last")
            to_side(g + 1, group)
    for load in loads[7:]:
        load.start()

    for load in loads[3:7]:
        load.wait()
    held = jnp.broadcast_to(tmap[...].astype(F32).reshape(1, 128), (128, 128)).T
    student_map = smap[...].astype(F32).reshape(1, 128)
    down = lax.broadcasted_iota(jnp.int32, (128, 128), 0).astype(F32)
    found = jnp.max(jnp.where(held == student_map, down, 0.0), axis=0, keepdims=True)
    order_vec[...] = jnp.broadcast_to(found, (8, 128)).astype(jnp.int32)
    load_order = pltpu.make_async_copy(order_vec, order_ref, lsem.at[9])
    load_order.start()

    two = ((1, pl.ds(0, 2)), (3, pl.ds(2, 2)))

    def pass_heavy(g, which=parts):
        for p in which:
            c = axes(p)[2]
            for d, half in two:
                from_c = moved(c, 4 - d)
                group = at(p, ALL, offset_b(p, g), from_c)
                arrived(group, "heavy", last_no(p, g, d))
                piece = at(p, half, offset_b(p, g), from_c)
                send(piece, piece, line(c, d), "halves", p * 4 + g, "last")
                to_side(g, group)

    def pass_halves(g):
        for p in parts:
            c = axes(p)[2]
            group = at(p, ALL, offset_b(p, g), moved(c, 2))
            arrived(group, "halves", p * 4 + g)
            to_side(g, group)

    pass_heavy(0)
    add_stats(1)
    spread_stats(2)
    for d, half, n in ways[:2]:
        piece = chunk(4 - d, half)
        arrived(piece, "ring", n)
        send(piece, piece, line(X, d), "far", 0, "ring")
        to_stud_side(piece)
    pass_heavy(1)
    for d, half, n in ways[2:]:
        piece = chunk(4 - d, half)
        arrived(piece, "ring", n)
        to_stud_side(piece)
    pass_halves(0)
    arrived(chunk(2), "far")
    to_stud_side(chunk(2))
    add_stats(2)
    send(st_own.at[3], st_rcv.at[9], sibling, "stats", 3)
    pass_heavy(2)
    pass_halves(1)

    sub = lax.broadcasted_iota(jnp.int32, (8, 128), 0)
    lane = lax.broadcasted_iota(jnp.int32, (8, 128), 1)
    pair = sub // 2

    def fill_messages(source, which, r, index):
        rows = source[pl.ds(pl.multiple_of(r * 8, 8), 8), :]
        tiles = shuffle4([rows[:, j * 128 : (j + 1) * 128] for j in range(4)], pair)
        for k in range(4):
            which[index(r, jnp.int32(k))] = tiles[k].astype(BF16)

    role_at = [div(moved(Y, b), 2) for b in range(4)]
    y_at = [rem(moved(Y, b), 2) * 8 for b in range(4)]
    x_at = [moved(X, a) * 16 for a in range(4)]
    z_at = [moved(Z, c) * 2 for c in range(4)]
    c_at = [me_c, 1 - me_c]
    near_last = sorted(
        ((a, c, e) for a in range(4) for c in range(4) for e in range(2)),
        key=lambda place: (-min(place[0], 4 - place[0]) - min(place[1], 4 - place[1]), -place[2]),
    )

    def send_plane(snd, rcv, sem, b):
        for a, c, e in near_last:
            if (a, b, c, e) != (0, 0, 0, 0):
                vocab_to = x_at[a] + y_at[b] + z_at[c] + c_at[e]
                pltpu.make_async_remote_copy(
                    snd.at[role_at[b] * 64 + vocab_to],
                    rcv.at[flat],
                    bulk_s.at[sem],
                    bulk_r.at[sem],
                    device_id=(role_at[b], vocab_to),
                    device_id_type=MESH,
                ).start()

    planes = (2, 1, 3, 0)

    def column_index(r, k):
        g = div(r, 2)
        return flat_of(rem(r, 2) * 2 + div(k, 2), div(g, 4), rem(g, 4), rem(k, 2))

    def plain_index(r, k):
        return r * 4 + k

    def bulk_wait(buf, sems, sem):
        pltpu.make_async_copy(buf.at[pl.ds(0, 127)], buf.at[pl.ds(0, 127)], sems.at[sem]).wait()

    arrived(st_rcv.at[9], "stats", 3)
    for r in range(2):
        total = st_own[3, r] + st_rcv[9, r]
        scale = lax.rsqrt(total * (1.0 / 16384) + EPS)
        scale_ref[r] = jnp.broadcast_to(scale[0:1], (128, 128)).T
    load_th.wait()
    acc[...] = jnp.zeros_like(acc)

    def teacher_step(dx, dz):
        x, z = rem(me[X] + dx, 4), rem(me[Z] + dz, 4)
        lanes, heads = [], []
        for y_lo in range(2):
            base = pl.multiple_of(x * 4096 + y_lo * 2048 + z * 512, 512)
            gain = tg[pl.ds(base, 512)].astype(F32).reshape(1, 512)
            heads.append(th[:, pl.ds(base, 512)])
            for c in range(2):
                rows = []
                for r in range(2):
                    block = gath[x, 2 * r + y_lo, z, c].astype(F32)
                    scale = scale_ref[r]
                    scale = jnp.concatenate([scale, scale], axis=1)
                    rows.append((block * scale * gain[:, c * 256 : (c + 1) * 256]).astype(BF16))
                lanes.append(jnp.concatenate(rows, axis=0))
        acc[...] += lax.dot_general(
            jnp.concatenate(lanes, axis=1),
            jnp.concatenate(heads, axis=1),
            (((1,), (1,)), ((), ())),
            preferred_element_type=F32,
        )

    arrived(gath.at[pl.ds(0, 2), :, :, 0], "side", 0)

    @pl.loop(0, 4)
    def _(i):
        teacher_step(3 * div(i, 2), 3 * rem(i, 2))

    pass_heavy(3)
    pass_halves(2)

    arrived(rows_a.at[pl.ds(0, 4)], "stud_side")
    load_sh.wait()
    for j in range(8):
        part = lax.dot_general(
            rows_a[j].reshape(256, 512),
            sh[:, j * 512 : (j + 1) * 512],
            (((1,), (1,)), ((), ())),
            preferred_element_type=F32,
        )
        if j == 0:
            acc_s[...] = part
        else:
            acc_s[...] += part

    @pl.loop(0, 32, unroll=4)
    def _(r):
        fill_messages(acc_s, sl_snd, r, column_index)

    sl_rcv[flat] = sl_snd[flat]

    for b in planes:
        send_plane(sl_snd, sl_rcv, 0, b)
    pass_halves(3)
    outs = [pltpu.make_async_copy(rows_a, rows_out, lsem.at[10])]
    outs[0].start()

    arrived(gath.at[0, :, :, 0], "side", 1)

    @pl.loop(0, 2)
    def _(i):
        teacher_step(3 * i, 1)

    @pl.loop(0, 3)
    def _(i):
        teacher_step(1, i + div(i, 2))

    arrived(gath.at[0, :, :, 0], "side", 2)

    @pl.loop(0, 4)
    def _(i):
        teacher_step(2, i)

    @pl.loop(0, 3)
    def _(q):
        teacher_step(q + div(q, 2), 2)

    for b in planes:
        base = role_at[b] * 16 + div(y_at[b], 4)

        @pl.loop(0, 8, unroll=4)
        def _(i, base=base):
            fill_messages(acc, tl_snd, base + i + 2 * div(i, 2), plain_index)

        send_plane(tl_snd, tl_rcv, 1, b)
    tl_rcv[flat] = tl_snd[flat]

    def over(value, op, reduce):
        value = jnp.broadcast_to(reduce(value, axis=1, keepdims=True), (8, 128))
        value = op(value, pltpu.roll(value, 2, 0))
        return op(value, pltpu.roll(value, 4, 0))

    def log_sum(ref):
        def top_step(i, top):
            return jnp.maximum(top, jnp.max(ref[pl.ds(i * 16, 16)].astype(F32), axis=0))

        top = lax.fori_loop(0, 8, top_step, jnp.full((8, 128), -jnp.inf, F32))
        top = over(top, jnp.maximum, jnp.max)

        def sum_step(i, total):
            part = jnp.exp(ref[pl.ds(i * 16, 16)].astype(F32) - top[None])
            return total + jnp.sum(part, axis=0)

        total = lax.fori_loop(0, 8, sum_step, jnp.zeros((8, 128), F32))
        return top + jnp.log(over(total, jnp.add, jnp.sum))

    load_order.wait()
    bulk_wait(sl_rcv, bulk_r, 0)
    stud_log = log_sum(sl_rcv)
    bulk_wait(tl_rcv, bulk_r, 1)
    teach_log = log_sum(tl_rcv)
    token = sub % 2
    lane_row = lax.broadcasted_iota(jnp.int32, (1, 128), 1).astype(F32)

    def label_place(label):
        block = div(label, 512)
        match = smap[...].astype(F32).reshape(1, 128) == block.astype(F32)
        place = jnp.sum(jnp.where(match, lane_row, 0.0), axis=1, keepdims=True)
        return place.astype(jnp.int32) * 512 + (label - block * 512)

    wanted = jnp.where(token == 0, label_place(ids[flat * 2]), label_place(ids[flat * 2 + 1]))
    place = pair * 128 + lane

    def term(i, carry):
        teach = tl_rcv[jnp.clip(order_ref[0, i], 0, 127)].astype(F32)
        student = sl_rcv[i].astype(F32)
        teach_prob = jnp.exp(teach - teach_log)
        stud_prob = jnp.exp(student - stud_log)
        hit = (place + i * 512) == wanted
        grad = LOSS_SCALE * (
            (1.0 + CE_WEIGHT) * stud_prob - teach_prob - CE_WEIGHT * hit.astype(F32)
        )
        g_snd[i] = grad.astype(BF16)
        return carry + teach_prob * (teach - student) - CE_WEIGHT * jnp.where(hit, student, 0.0)

    total = jnp.zeros((8, 128), F32)
    for b in planes:
        base = role_at[b] * 64 + y_at[b]
        total = lax.fori_loop(
            0, 32, lambda j, carry, base=base: term(base + j + 8 * div(j, 8), carry), total, unroll=8
        )
        send_plane(g_snd, g_rcv, 2, b)
    g_rcv[flat] = g_snd[flat]
    once = (sub < 2) & (lane == 0)
    total = total + jnp.where(once, (1.0 + CE_WEIGHT) * stud_log - teach_log, 0.0)
    total = jnp.sum(jnp.sum(total, axis=1, keepdims=True), axis=0, keepdims=True)
    ls_own[0] = jnp.broadcast_to(total, (8, 128))
    send(ls_own.at[0], ls_rcv.at[0], sibling, "loss", 0)

    def add_loss(stage):
        base = 4 * stage - 3
        axis = (Y, Z, X)[stage - 1]
        arrived(ls_rcv.at[pl.ds(base, 3)], "loss", stage)
        total = jnp.zeros((8, 128), F32)
        for i in range(4):
            total = total + jnp.where(me[axis] == i, ls_own[stage], ls_rcv[base + i])
        ls_own[stage + 1] = total

    def spread_loss(stage):
        base = 4 * stage - 3
        axis = (Y, Z, X)[stage - 1]
        for d in steps:
            send(ls_own.at[stage], ls_rcv.at[base + me[axis]], line(axis, d), "loss", stage)

    for i in range(3):
        ls_rcv[1 + 4 * i + me[(Y, Z, X)[i]]] = jnp.zeros((8, 128), F32)
    arrived(ls_rcv.at[0], "loss", 0)
    ls_own[1] = ls_own[0] + ls_rcv[0]
    spread_loss(1)

    bulk_wait(g_rcv, bulk_r, 2)

    @pl.loop(0, 16)
    def _(g):
        rows = []
        for h in range(2):
            msgs = [g_rcv[column_index(g * 2 + h, k)].astype(F32) for k in range(4)]
            rows.append(jnp.concatenate(shuffle4(msgs, pair), axis=1))
        start = pl.multiple_of(g * 16, 16)
        g2_ref[pl.ds(start, 16), :] = jnp.concatenate(rows, axis=0).astype(BF16)

    def hidden_cols(core, part):
        cols = pl.ds(pl.multiple_of(core * 2048 + part * 512, 512), 512)
        value = jnp.dot(g2_ref[...], sh[:, cols], preferred_element_type=F32)
        return value.reshape(4, 4, 16, 512)

    for part in range(4):
        sib_snd[part] = hidden_cols(1 - me_c, part).astype(BF16)
        send(sib_snd.at[part], sib_rcv.at[part], sibling, "sib", part)
    for part in range(4):
        hb[part] = hidden_cols(me_c, part)
    add_loss(1)
    spread_loss(2)

    for part in range(4):
        axis = (Y, Z)[part % 2]
        arrived(sib_rcv.at[part], "sib", part)
        summed = hb[part] + sib_rcv[part].astype(F32)
        hb[part] = summed
        p1_snd[part] = (summed if axis == Y else jnp.swapaxes(summed, 0, 1)).astype(BF16)
        for i, d in enumerate(steps):
            send(p1_snd.at[part, moved(axis, d)], p1_rcv.at[part, i], line(axis, d), "line", part)

    g2t[...] = g2_ref[...].astype(F32).T.astype(BF16)
    outs.append(pltpu.make_async_copy(g2t, g2t_out, lsem.at[11]))
    outs[1].start()
    add_loss(2)
    spread_loss(3)

    for way, axis in enumerate((Y, Z)):
        for h in range(2):
            part = way + 2 * h
            total = hb[part, me[Y]] if axis == Y else hb[part, :, me[Z]]
            arrived(p1_rcv.at[part], "line", part)
            for i in range(3):
                total = total + p1_rcv[part, i].astype(F32)
            for q in range(4):
                for k in range(8):
                    p2_snd[way, q * 8 + k, :, h * 512 : (h + 1) * 512] = total[q, 2 * k : 2 * k + 2].astype(BF16)
        own = (me[Z] if axis == Y else me[Y]) * 8 + j_me
        p2_rcv[way, own] = p2_snd[way, own]
        other = Z if axis == Y else Y
        for a, o, e in near_last:
            if (a, o, e) == (0, 0, 0):
                continue
            q, x, c = moved(other, o), moved(X, a), c_at[e]
            to = q * 8 + x * 2 + c
            y, z = (me[Y], q) if axis == Y else (q, me[Z])
            send(
                p2_snd.at[way, to], p2_rcv.at[way, own], device(x, y, z, c), "direct", way
            )
    for way in range(2):
        arrived(p2_rcv.at[way, pl.ds(0, 31)], "direct", way)
    back = []
    for c in range(2):
        sums = []
        for way in range(2):
            total = jnp.zeros((2, 1024), F32)
            for k in range(16):
                total = total + p2_rcv[way, k * 2 + c].astype(F32)
            sums.append(total)
        for part in range(4):
            back.append(sums[part % 2][:, part // 2 * 512 : (part // 2 + 1) * 512])
    back = jnp.concatenate(back, axis=1) * sg[...].astype(F32).reshape(1, 4096)
    hat = s_ref[...].astype(F32) * stud_scale
    ig_ref[...] = stud_scale * (back - hat * jnp.mean(back * hat, axis=1, keepdims=True))
    add_loss(3)
    loss_ref[0, 0] = jnp.sum(jnp.where((sub == 0) & (lane == 0), ls_own[4], 0.0)) * (1.0 / 256)

    for out in outs:
        out.wait()
    left(s_snd.at[pl.ds(0, 7)], "spread")
    left(rows_a.at[0, pl.ds(0, 15)], "plane")
    left(rows_a.at[pl.ds(0, 3)], "ring")
    left(rows_a.at[pl.ds(0, 4)], "stud_side")
    left(gath.at[0, 0, pl.ds(0, 3), 0], "first")
    left(gath.at[0, pl.ds(0, 3), :, 0], "second")
    left(gath.at[pl.ds(0, 3), :, :, 0], "last")
    left(gath.at[:, :, :, 0], "side")
    left(st_rcv, "stats")
    left(ls_rcv.at[pl.ds(0, 10)], "loss")
    left(sib_snd, "sib")
    left(p1_snd.at[:, pl.ds(0, 3)], "line")
    left(p2_snd.at[:, pl.ds(0, 31)], "direct")
    for k, buf in enumerate((sl_snd, tl_snd, g_snd)):
        bulk_wait(buf, bulk_s, k)


def head_kernel(grad_hbm, rows_hbm, ig_hbm, out_hbm, ig_out, grad, rows, out, sems):
    move_ig = pltpu.make_async_copy(ig_hbm, ig_out, sems.at[17])
    move_ig.start()
    load_grad = pltpu.make_async_copy(grad_hbm, grad, sems.at[16])
    load_grad.start()
    loads, stores = [], []
    for j in range(8):
        loads.append(pltpu.make_async_copy(rows_hbm.at[j], rows.at[j], sems.at[j]))
        loads[j].start()
    load_grad.wait()
    for j in range(8):
        cols = pl.ds(j * 512, 512)
        loads[j].wait()
        out[:, cols] = jnp.dot(
            grad[...], rows[j].reshape(256, 512), preferred_element_type=F32
        ).astype(BF16)
        stores.append(pltpu.make_async_copy(out.at[:, cols], out_hbm.at[:, cols], sems.at[8 + j]))
        stores[j].start()
    for store in stores:
        store.wait()
    move_ig.wait()


def body(
    teacher_hidden,
    teacher_gain,
    teacher_head,
    student_hidden,
    student_gain,
    student_head,
    token_ids,
    teacher_map,
    student_map,
):
    vmem = pl.BlockSpec(memory_space=pltpu.VMEM)
    hbm = pl.BlockSpec(memory_space=pltpu.HBM)
    loss, input_grad, grad, rows = pl.pallas_call(
        kernel,
        out_shape=(
            jax.ShapeDtypeStruct((1, 1), F32),
            jax.ShapeDtypeStruct((2, 4096), F32),
            jax.ShapeDtypeStruct((512, 256), BF16),
            jax.ShapeDtypeStruct((8, 16, 16, 512), BF16),
        ),
        in_specs=[hbm] * 9,
        out_specs=(pl.BlockSpec(memory_space=pltpu.SMEM), vmem, hbm, hbm),
        scratch_shapes=[
            pltpu.VMEM((4, 4, 4, 2, 128, 256), BF16),
            pltpu.VMEM((512, 16384), BF16),
            pltpu.VMEM((512, 4096), BF16),
            pltpu.VMEM((16384,), BF16),
            pltpu.VMEM((4096,), BF16),
            pltpu.VMEM((2, 4096), BF16),
            pltpu.VMEM((128,), jnp.int32),
            pltpu.VMEM((128,), jnp.int32),
            pltpu.VMEM((8, 128), jnp.int32),
            pltpu.SMEM((256,), jnp.int32),
            pltpu.SMEM((8, 128), jnp.int32),
            pltpu.VMEM((256, 512), F32),
            pltpu.VMEM((256, 512), F32),
            pltpu.VMEM((8, 16, 16, 512), BF16),
            pltpu.VMEM((8, 2, 512), BF16),
            pltpu.VMEM((8, 2, 512), BF16),
            pltpu.VMEM((5, 2, 8, 128), F32),
            pltpu.VMEM((10, 2, 8, 128), F32),
            pltpu.VMEM((2, 128, 128), F32),
            pltpu.VMEM((128, 8, 128), BF16),
            pltpu.VMEM((128, 8, 128), BF16),
            pltpu.VMEM((128, 8, 128), BF16),
            pltpu.VMEM((128, 8, 128), BF16),
            pltpu.VMEM((128, 8, 128), BF16),
            pltpu.VMEM((128, 8, 128), BF16),
            pltpu.VMEM((256, 512), BF16),
            pltpu.VMEM((512, 256), BF16),
            pltpu.VMEM((4, 4, 4, 16, 512), BF16),
            pltpu.VMEM((4, 4, 4, 16, 512), BF16),
            pltpu.VMEM((4, 4, 4, 16, 512), F32),
            pltpu.VMEM((4, 4, 4, 16, 512), BF16),
            pltpu.VMEM((4, 3, 4, 16, 512), BF16),
            pltpu.VMEM((2, 32, 2, 1024), BF16),
            pltpu.VMEM((2, 32, 2, 1024), BF16),
            pltpu.VMEM((5, 8, 128), F32),
            pltpu.VMEM((13, 8, 128), F32),
            pltpu.SemaphoreType.DMA((len(SEND),)),
            pltpu.SemaphoreType.DMA((N_RECV,)),
            pltpu.SemaphoreType.DMA((12,)),
            pltpu.SemaphoreType.DMA((3,)),
            pltpu.SemaphoreType.DMA((3,)),
        ],
        compiler_params=pltpu.CompilerParams(
            collective_id=0, has_side_effects=True, vmem_limit_bytes=63 << 20
        ),
        cost_estimate=pl.CostEstimate(
            flops=2 * 256 * 512 * (16384 + 3 * 4096), bytes_accessed=24 << 20, transcendentals=0
        ),
        name="distill",
    )(
        teacher_hidden,
        teacher_gain,
        teacher_head,
        student_hidden,
        student_gain,
        student_head,
        token_ids,
        teacher_map,
        student_map,
    )
    head_grad, input_grad = pl.pallas_call(
        head_kernel,
        out_shape=(
            jax.ShapeDtypeStruct((512, 4096), BF16),
            jax.ShapeDtypeStruct((2, 4096), F32),
        ),
        in_specs=[hbm, hbm, hbm],
        out_specs=(hbm, hbm),
        scratch_shapes=[
            pltpu.VMEM((512, 256), BF16),
            pltpu.VMEM((8, 16, 16, 512), BF16),
            pltpu.VMEM((512, 4096), BF16),
            pltpu.SemaphoreType.DMA((18,)),
        ],
        compiler_params=pltpu.CompilerParams(vmem_limit_bytes=63 << 20),
        cost_estimate=pl.CostEstimate(
            flops=2 * 256 * 512 * 4096, bytes_accessed=6 << 20, transcendentals=0
        ),
        name="head",
    )(grad, rows, input_grad)
    return (loss.reshape(()), head_grad, input_grad)


def solution(mesh):
    placed = (
        P("role", "vocab"),
        P(),
        P(("role", "vocab"), None),
        P(("role", "vocab"), None),
        P(),
        P(("role", "vocab"), None),
        P(),
        P(),
        P(),
    )
    return jax.shard_map(
        body,
        mesh=mesh,
        in_specs=placed,
        out_specs=(P(), P(("role", "vocab"), None), P(("role", "vocab"), None)),
        check_vma=False,
    )
```

```python
import jax
import jax.numpy as jnp
from jax import lax
from jax.experimental import pallas as pl
from jax.experimental.pallas import tpu as pltpu
from jax.sharding import PartitionSpec as P

EPS = 1e-05
LOSS_SCALE = 256.0
CE_WEIGHT = 0.25
MESH = pl.DeviceIdType.MESH
F32 = jnp.float32
BF16 = jnp.bfloat16
X, Y, Z = 0, 1, 2
ALL = pl.ds(0, 4)
PARTS = (((Y, Z, X), 0, 32), ((X, Z, Y), 32, 48), ((Y, X, Z), 80, 48))
SEND = {name: k for k, name in enumerate(
    ("spread", "plane", "ring", "stud_side", "first", "second", "last", "side", "stats", "loss", "sib", "line", "direct")
)}
RECV_COUNTS = dict(
    spread=1, plane=1, ring=4, far=1, stud_side=1, first=9, second=9, heavy=24, halves=4,
    side=3, stats=4, loss=4, sib=4, line=4, direct=2,
)
RECV = {name: sum(list(RECV_COUNTS.values())[:k]) for k, name in enumerate(RECV_COUNTS)}
N_RECV = sum(RECV_COUNTS.values())


def div(a, b):
    return lax.div(a, jnp.int32(b))


def rem(a, b):
    return lax.rem(a, jnp.int32(b))


def flat_of(x, y, z, c):
    return div(y, 2) * 64 + ((x * 2 + rem(y, 2)) * 4 + z) * 2 + c


def shuffle4(tiles, pair):
    out = []
    for b in range(4):
        acc = None
        for a in range(4):
            shift = (2 * (a - b)) % 8
            moved = pltpu.roll(tiles[a], shift, 0) if shift else tiles[a]
            acc = moved if acc is None else jnp.where(pair == a, moved, acc)
        out.append(acc)
    return out


def kernel(
    t_hbm,
    tg_hbm,
    th_hbm,
    s_hbm,
    sg_hbm,
    sh_hbm,
    ids_hbm,
    tm_hbm,
    sm_hbm,
    loss_ref,
    ig_ref,
    g2t_out,
    rows_out,
    gath,
    th,
    sh,
    tg,
    sg,
    s_ref,
    tmap,
    smap,
    order_vec,
    ids,
    order_ref,
    acc,
    acc_s,
    rows_a,
    s_snd,
    s_rcv,
    st_own,
    st_rcv,
    scale_ref,
    tl_snd,
    tl_rcv,
    sl_snd,
    sl_rcv,
    g_snd,
    g_rcv,
    g2_ref,
    g2t,
    sib_snd,
    sib_rcv,
    hb,
    p1_snd,
    p1_rcv,
    p2_snd,
    p2_rcv,
    ls_own,
    ls_rcv,
    ssem,
    rsem,
    lsem,
    bulk_s,
    bulk_r,
):
    role = lax.axis_index("role")
    vocab = lax.axis_index("vocab")
    me_c = rem(vocab, 2)
    me = (div(vocab, 16), role * 2 + rem(div(vocab, 8), 2), rem(div(vocab, 2), 4))
    flat = role * 64 + vocab
    j_me = me[X] * 2 + me_c
    g_me = me[Y] * 4 + me[Z]

    def device(x, y, z, c):
        return (div(y, 2), ((x * 2 + rem(y, 2)) * 4 + z) * 2 + c)

    def moved(axis, step):
        return rem(me[axis] + step, 4)

    def line(axis, step):
        at = list(me)
        at[axis] = moved(axis, step)
        return device(at[0], at[1], at[2], me_c)

    sibling = device(me[X], me[Y], me[Z], 1 - me_c)

    def column(k):
        return device(div(k, 2), me[Y], me[Z], rem(k, 2))

    def plane(dy, dz):
        return device(me[X], moved(Y, dy), moved(Z, dz), me_c)

    def send(src, dst, to, group, index=0, sender=None):
        pltpu.make_async_remote_copy(
            src,
            dst,
            ssem.at[SEND[sender or group]],
            rsem.at[RECV[group] + index],
            device_id=to,
            device_id_type=MESH,
        ).start()

    def arrived(ref, group, index=0):
        pltpu.make_async_copy(ref, ref, rsem.at[RECV[group] + index]).wait()

    def left(ref, sender):
        pltpu.make_async_copy(ref, ref, ssem.at[SEND[sender]]).wait()

    plane_steps = [(dy, dz) for dy in range(4) for dz in range(4) if (dy, dz) != (0, 0)]
    barrier = pltpu.get_barrier_semaphore()
    for k in range(1, 8):
        pl.semaphore_signal(barrier, inc=1, device_id=column(rem(j_me + k, 8)), device_id_type=MESH)
    for dy, dz in plane_steps:
        pl.semaphore_signal(barrier, inc=1, device_id=plane(dy, dz), device_id_type=MESH)

    own_slot = gath.at[me[X], me[Y], me[Z], me_c]
    loads = [
        pltpu.make_async_copy(src, dst, lsem.at[k])
        for k, (src, dst) in enumerate(
            (
                (t_hbm, own_slot),
                (s_hbm, s_ref),
                (sg_hbm, sg),
                (tg_hbm, tg),
                (tm_hbm, tmap),
                (sm_hbm, smap),
                (ids_hbm, ids),
                (sh_hbm, sh),
                (th_hbm, th),
            )
        )
    ]
    for load in loads[:7]:
        load.start()
    load_sh, load_th = loads[7:]

    loads[1].wait()
    loads[2].wait()
    stud = s_ref[...].astype(F32)
    stud_gain = sg[...].astype(F32).reshape(1, 4096)
    stud_scale = lax.rsqrt(jnp.mean(stud * stud, axis=1, keepdims=True) + EPS)
    stud_normed = (stud * stud_scale * stud_gain).astype(BF16)
    for j in range(8):
        s_snd[j] = stud_normed[:, j * 512 : (j + 1) * 512]
    s_rcv[j_me] = s_snd[j_me]
    loads[0].wait()
    own_f = own_slot[...].astype(F32)
    sums = jnp.sum(own_f * own_f, axis=1, keepdims=True)
    flipped = jnp.broadcast_to(sums, (128, 128)).T[:8]
    st_own[0, 0] = jnp.where(role == 0, flipped, 0.0)
    st_own[0, 1] = jnp.where(role == 1, flipped, 0.0)

    pl.semaphore_wait(barrier, 22)

    def at(part, a, b, c):
        (first, second, last), start, count = PARTS[part]
        index = [None, None, None]
        index[first], index[second], index[last] = a, b, c
        return gath.at[index[0], index[1], index[2], me_c, pl.ds(start, count)]

    def axes(part):
        return PARTS[part][0]

    parts = range(3)
    steps = (1, 3, 2)

    for k in range(1, 8):
        to = rem(j_me + k, 8)
        send(s_snd.at[to], s_rcv.at[j_me], column(to), "spread")

    def no(p, d):
        return p * 3 + steps.index(d)

    def last_no(p, g, d):
        return (p * 4 + g) * 2 + d // 2

    def mine(p):
        a, b, c = axes(p)
        return at(p, me[a], me[b], me[c])

    for p in parts:
        a, b, c = axes(p)
        for d in steps:
            send(mine(p), mine(p), line(a, d), "first", no(p, d))
    for p in parts:
        a, b, c = axes(p)
        for d in (1, 3):
            send(mine(p), mine(p), line(c, d), "heavy", last_no(p, 0, d), "last")
        for d in steps:
            send(mine(p), mine(p), line(b, d), "second", no(p, d))
    def spread_stats(stage):
        for i, d in enumerate(steps):
            send(st_own.at[stage], st_rcv.at[stage * 3 + i], line((X, Y, Z)[stage], d), "stats", stage)

    def add_stats(stage):
        arrived(st_rcv.at[pl.ds(stage * 3, 3)], "stats", stage)
        total = st_own[stage]
        for i in range(3):
            total = total + st_rcv[stage * 3 + i]
        st_own[stage + 1] = total

    spread_stats(0)

    def to_side(g, ref):
        send(ref, ref, sibling, "side", max(g - 1, 0))

    def to_stud_side(ref):
        send(ref, ref, sibling, "stud_side")

    def offset_b(p, g):
        return moved(axes(p)[1], (0, 3, 1, 2)[g])

    arrived(s_rcv.at[pl.ds(0, 7)], "spread")
    tile = jnp.concatenate([s_rcv[k].astype(F32) for k in range(8)], axis=0)
    rows_a[j_me, g_me] = tile.astype(BF16)
    tile_ref = rows_a.at[j_me, g_me]
    for dy, dz in plane_steps:
        send(tile_ref, tile_ref, plane(dy, dz), "plane")

    for d in steps:
        for p in parts:
            a, b, c = axes(p)
            block = at(p, moved(a, 4 - d), me[b], me[c])
            arrived(block, "first", no(p, d))
            for e in steps:
                send(block, block, line(b, e), "second", no(p, e))
            for e in (1, 3):
                send(block, block, line(c, e), "heavy", last_no(p, 0, e), "last")
    for p in parts:
        a, b, c = axes(p)
        to_side(0, at(p, ALL, me[b], me[c]))

    low, high = pl.ds(0, 8), pl.ds(8, 8)
    ways = ((1, low, 0), (3, high, 1), (1, high, 2), (3, low, 3))

    def chunk(step, half=pl.ds(0, 16)):
        return rows_a.at[moved(X, step) * 2 + me_c, half]

    arrived(rows_a.at[j_me, pl.ds(0, 15)], "plane")
    for d, half, n in ways:
        send(chunk(0, half), chunk(0, half), line(X, d), "ring", n)
    to_stud_side(chunk(0))
    add_stats(0)
    spread_stats(1)

    for g, d in enumerate(steps):
        for p in parts:
            a, b, c = axes(p)
            group = at(p, ALL, offset_b(p, g + 1), me[c])
            arrived(group, "second", no(p, d))
            for e in (1, 3):
                send(group, group, line(c, e), "heavy", last_no(p, g + 1, e), "last")
            to_side(g + 1, group)
    for load in loads[7:]:
        load.start()

    for load in loads[3:7]:
        load.wait()
    held = jnp.broadcast_to(tmap[...].astype(F32).reshape(1, 128), (128, 128)).T
    student_map = smap[...].astype(F32).reshape(1, 128)
    down = lax.broadcasted_iota(jnp.int32, (128, 128), 0).astype(F32)
    found = jnp.max(jnp.where(held == student_map, down, 0.0), axis=0, keepdims=True)
    order_vec[...] = jnp.broadcast_to(found, (8, 128)).astype(jnp.int32)
    load_order = pltpu.make_async_copy(order_vec, order_ref, lsem.at[9])
    load_order.start()

    two = ((1, pl.ds(0, 2)), (3, pl.ds(2, 2)))

    def pass_heavy(g, which=parts):
        for p in which:
            c = axes(p)[2]
            for d, half in two:
                from_c = moved(c, 4 - d)
                group = at(p, ALL, offset_b(p, g), from_c)
                arrived(group, "heavy", last_no(p, g, d))
                piece = at(p, half, offset_b(p, g), from_c)
                send(piece, piece, line(c, d), "halves", g, "last")
                to_side(g, group)

    def pass_halves(g):
        arrived(gath.at[0, 0, :, 0], "halves", g)
        for p in parts:
            to_side(g, at(p, ALL, offset_b(p, g), moved(axes(p)[2], 2)))

    pass_heavy(0)
    add_stats(1)
    spread_stats(2)
    for d, half, n in ways[:2]:
        piece = chunk(4 - d, half)
        arrived(piece, "ring", n)
        send(piece, piece, line(X, d), "far", 0, "ring")
        to_stud_side(piece)
    pass_heavy(1)
    for d, half, n in ways[2:]:
        piece = chunk(4 - d, half)
        arrived(piece, "ring", n)
        to_stud_side(piece)
    pass_halves(0)
    arrived(chunk(2), "far")
    to_stud_side(chunk(2))
    add_stats(2)
    send(st_own.at[3], st_rcv.at[9], sibling, "stats", 3)
    pass_heavy(2)
    pass_halves(1)

    sub = lax.broadcasted_iota(jnp.int32, (8, 128), 0)
    lane = lax.broadcasted_iota(jnp.int32, (8, 128), 1)
    pair = sub // 2

    def fill_messages(source, which, r, index):
        rows = source[pl.ds(pl.multiple_of(r * 8, 8), 8), :]
        tiles = shuffle4([rows[:, j * 128 : (j + 1) * 128] for j in range(4)], pair)
        for k in range(4):
            which[index(r, jnp.int32(k))] = tiles[k].astype(BF16)

    role_at = [div(moved(Y, b), 2) for b in range(4)]
    y_at = [rem(moved(Y, b), 2) * 8 for b in range(4)]
    x_at = [moved(X, a) * 16 for a in range(4)]
    z_at = [moved(Z, c) * 2 for c in range(4)]
    c_at = [me_c, 1 - me_c]
    near_last = sorted(
        ((a, c, e) for a in range(4) for c in range(4) for e in range(2)),
        key=lambda place: (-min(place[0], 4 - place[0]) - min(place[1], 4 - place[1]), -place[2]),
    )

    def send_plane(snd, rcv, sem, b):
        for a, c, e in near_last:
            if (a, b, c, e) != (0, 0, 0, 0):
                vocab_to = x_at[a] + y_at[b] + z_at[c] + c_at[e]
                pltpu.make_async_remote_copy(
                    snd.at[role_at[b] * 64 + vocab_to],
                    rcv.at[flat],
                    bulk_s.at[sem],
                    bulk_r.at[sem],
                    device_id=(role_at[b], vocab_to),
                    device_id_type=MESH,
                ).start()

    planes = (2, 1, 3, 0)

    def column_index(r, k):
        g = div(r, 2)
        return flat_of(rem(r, 2) * 2 + div(k, 2), div(g, 4), rem(g, 4), rem(k, 2))

    def plain_index(r, k):
        return r * 4 + k

    def bulk_wait(buf, sems, sem):
        pltpu.make_async_copy(buf.at[pl.ds(0, 127)], buf.at[pl.ds(0, 127)], sems.at[sem]).wait()

    arrived(st_rcv.at[9], "stats", 3)
    for r in range(2):
        total = st_own[3, r] + st_rcv[9, r]
        scale = lax.rsqrt(total * (1.0 / 16384) + EPS)
        scale_ref[r] = jnp.broadcast_to(scale[0:1], (128, 128)).T
    load_th.wait()
    acc[...] = jnp.zeros_like(acc)

    def teacher_step(*places):
        lanes, heads = [], []
        for x, z, y_lo in (
            (rem(me[X] + dx, 4), rem(me[Z] + dz, 4), y_lo) for dx, dz in places for y_lo in range(2)
        ):
            base = pl.multiple_of(x * 4096 + y_lo * 2048 + z * 512, 512)
            gain = tg[pl.ds(base, 512)].astype(F32).reshape(1, 512)
            heads.append(th[:, pl.ds(base, 512)])
            for c in range(2):
                rows = []
                for r in range(2):
                    block = gath[x, 2 * r + y_lo, z, c].astype(F32)
                    scale = scale_ref[r]
                    scale = jnp.concatenate([scale, scale], axis=1)
                    rows.append((block * scale * gain[:, c * 256 : (c + 1) * 256]).astype(BF16))
                lanes.append(jnp.concatenate(rows, axis=0))
        acc[...] += lax.dot_general(
            jnp.concatenate(lanes, axis=1),
            jnp.concatenate(heads, axis=1),
            (((1,), (1,)), ((), ())),
            preferred_element_type=F32,
        )

    arrived(gath.at[pl.ds(0, 2), :, :, 0], "side", 0)

    @pl.loop(0, 2)
    def _(i):
        teacher_step((3 * i, 0), (3 * i, 3))

    pass_heavy(3)
    pass_halves(2)

    arrived(rows_a.at[pl.ds(0, 4)], "stud_side")
    load_sh.wait()
    for j in range(2):
        part = lax.dot_general(
            jnp.concatenate([rows_a[4 * j + k].reshape(256, 512) for k in range(4)], axis=1),
            sh[:, j * 2048 : (j + 1) * 2048],
            (((1,), (1,)), ((), ())),
            preferred_element_type=F32,
        )
        if j == 0:
            acc_s[...] = part
        else:
            acc_s[...] += part

    @pl.loop(0, 32, unroll=8)
    def _(r):
        fill_messages(acc_s, sl_snd, r, column_index)

    sl_rcv[flat] = sl_snd[flat]

    for b in planes:
        send_plane(sl_snd, sl_rcv, 0, b)
    pass_halves(3)
    outs = [pltpu.make_async_copy(rows_a, rows_out, lsem.at[10])]
    outs[0].start()

    arrived(gath.at[0, :, :, 0], "side", 1)

    teacher_step((0, 1), (3, 1))
    teacher_step((1, 0), (1, 1), (1, 3))

    arrived(gath.at[0, :, :, 0], "side", 2)

    @pl.loop(0, 2)
    def _(i):
        teacher_step((2, 2 * i), (2, 2 * i + 1))

    teacher_step((0, 2), (1, 2), (3, 2))

    for b in planes:
        base = role_at[b] * 16 + div(y_at[b], 4)

        @pl.loop(0, 8, unroll=8)
        def _(i, base=base):
            fill_messages(acc, tl_snd, base + i + 2 * div(i, 2), plain_index)

        send_plane(tl_snd, tl_rcv, 1, b)
    tl_rcv[flat] = tl_snd[flat]

    def over(value, op, reduce):
        value = jnp.broadcast_to(reduce(value, axis=1, keepdims=True), (8, 128))
        value = op(value, pltpu.roll(value, 2, 0))
        return op(value, pltpu.roll(value, 4, 0))

    def log_sum(ref):
        def top_step(i, top):
            return jnp.maximum(top, jnp.max(ref[pl.ds(i * 16, 16)].astype(F32), axis=0))

        top = lax.fori_loop(0, 8, top_step, jnp.full((8, 128), -jnp.inf, F32), unroll=4)
        top = over(top, jnp.maximum, jnp.max)

        def sum_step(i, total):
            part = jnp.exp(ref[pl.ds(i * 16, 16)].astype(F32) - top[None])
            return total + jnp.sum(part, axis=0)

        total = lax.fori_loop(0, 8, sum_step, jnp.zeros((8, 128), F32), unroll=4)
        return top + jnp.log(over(total, jnp.add, jnp.sum))

    load_order.wait()
    bulk_wait(sl_rcv, bulk_r, 0)
    stud_log = log_sum(sl_rcv)
    bulk_wait(tl_rcv, bulk_r, 1)
    teach_log = log_sum(tl_rcv)
    token = sub % 2
    lane_row = lax.broadcasted_iota(jnp.int32, (1, 128), 1).astype(F32)

    def label_place(label):
        block = div(label, 512)
        match = smap[...].astype(F32).reshape(1, 128) == block.astype(F32)
        place = jnp.sum(jnp.where(match, lane_row, 0.0), axis=1, keepdims=True)
        return place.astype(jnp.int32) * 512 + (label - block * 512)

    wanted = jnp.where(token == 0, label_place(ids[flat * 2]), label_place(ids[flat * 2 + 1]))
    place = pair * 128 + lane

    def term(i, carry):
        teach = tl_rcv[jnp.clip(order_ref[0, i], 0, 127)].astype(F32)
        student = sl_rcv[i].astype(F32)
        teach_prob = jnp.exp(teach - teach_log)
        stud_prob = jnp.exp(student - stud_log)
        hit = (place + i * 512) == wanted
        grad = LOSS_SCALE * (
            (1.0 + CE_WEIGHT) * stud_prob - teach_prob - CE_WEIGHT * hit.astype(F32)
        )
        g_snd[i] = grad.astype(BF16)
        return carry + teach_prob * (teach - student) - CE_WEIGHT * jnp.where(hit, student, 0.0)

    total = jnp.zeros((8, 128), F32)
    for b in planes:
        base = role_at[b] * 64 + y_at[b]
        total = lax.fori_loop(
            0, 32, lambda j, carry, base=base: term(base + j + 8 * div(j, 8), carry), total, unroll=16
        )
        send_plane(g_snd, g_rcv, 2, b)
    g_rcv[flat] = g_snd[flat]
    once = (sub < 2) & (lane == 0)
    total = total + jnp.where(once, (1.0 + CE_WEIGHT) * stud_log - teach_log, 0.0)
    total = jnp.sum(jnp.sum(total, axis=1, keepdims=True), axis=0, keepdims=True)
    ls_own[0] = jnp.broadcast_to(total, (8, 128))
    send(ls_own.at[0], ls_rcv.at[0], sibling, "loss", 0)

    def add_loss(stage):
        base = 4 * stage - 3
        axis = (Y, Z, X)[stage - 1]
        arrived(ls_rcv.at[pl.ds(base, 3)], "loss", stage)
        total = jnp.zeros((8, 128), F32)
        for i in range(4):
            total = total + jnp.where(me[axis] == i, ls_own[stage], ls_rcv[base + i])
        ls_own[stage + 1] = total

    def spread_loss(stage):
        base = 4 * stage - 3
        axis = (Y, Z, X)[stage - 1]
        for d in steps:
            send(ls_own.at[stage], ls_rcv.at[base + me[axis]], line(axis, d), "loss", stage)

    for i in range(3):
        ls_rcv[1 + 4 * i + me[(Y, Z, X)[i]]] = jnp.zeros((8, 128), F32)
    arrived(ls_rcv.at[0], "loss", 0)
    ls_own[1] = ls_own[0] + ls_rcv[0]
    spread_loss(1)

    bulk_wait(g_rcv, bulk_r, 2)

    @pl.loop(0, 16, unroll=4)
    def _(g):
        rows = []
        for h in range(2):
            msgs = [g_rcv[column_index(g * 2 + h, k)].astype(F32) for k in range(4)]
            rows.append(jnp.concatenate(shuffle4(msgs, pair), axis=1))
        start = pl.multiple_of(g * 16, 16)
        g2_ref[pl.ds(start, 16), :] = jnp.concatenate(rows, axis=0).astype(BF16)

    def hidden_cols(core, part):
        cols = pl.ds(pl.multiple_of(core * 2048 + part * 512, 512), 512)
        value = jnp.dot(g2_ref[...], sh[:, cols], preferred_element_type=F32)
        return value.reshape(4, 4, 16, 512)

    for part in range(4):
        sib_snd[part] = hidden_cols(1 - me_c, part).astype(BF16)
        send(sib_snd.at[part], sib_rcv.at[part], sibling, "sib", part)
    for part in range(4):
        hb[part] = hidden_cols(me_c, part)
    add_loss(1)
    spread_loss(2)

    for part in range(4):
        axis = (Y, Z)[part % 2]
        arrived(sib_rcv.at[part], "sib", part)
        summed = hb[part] + sib_rcv[part].astype(F32)
        hb[part] = summed
        p1_snd[part] = (summed if axis == Y else jnp.swapaxes(summed, 0, 1)).astype(BF16)
        for i, d in enumerate((2, 1, 3)):
            send(p1_snd.at[part, moved(axis, d)], p1_rcv.at[part, i], line(axis, d), "line", part)

    g2t[...] = g2_ref[...].astype(F32).T.astype(BF16)
    outs.append(pltpu.make_async_copy(g2t, g2t_out, lsem.at[11]))
    outs[1].start()
    add_loss(2)
    spread_loss(3)

    for way, axis in enumerate((Y, Z)):
        for h in range(2):
            part = way + 2 * h
            total = hb[part, me[Y]] if axis == Y else hb[part, :, me[Z]]
            arrived(p1_rcv.at[part], "line", part)
            for i in range(3):
                total = total + p1_rcv[part, i].astype(F32)
            for q in range(4):
                for k in range(8):
                    p2_snd[way, q * 8 + k, :, h * 512 : (h + 1) * 512] = total[q, 2 * k : 2 * k + 2].astype(BF16)
        own = (me[Z] if axis == Y else me[Y]) * 8 + j_me
        p2_rcv[way, own] = p2_snd[way, own]
        other = Z if axis == Y else Y
        for a, o, e in near_last:
            if (a, o, e) == (0, 0, 0):
                continue
            q, x, c = moved(other, o), moved(X, a), c_at[e]
            to = q * 8 + x * 2 + c
            y, z = (me[Y], q) if axis == Y else (q, me[Z])
            send(
                p2_snd.at[way, to], p2_rcv.at[way, own], device(x, y, z, c), "direct", way
            )
    for way in range(2):
        arrived(p2_rcv.at[way, pl.ds(0, 31)], "direct", way)
    back = []
    for c in range(2):
        sums = []
        for way in range(2):
            total = jnp.zeros((2, 1024), F32)
            for k in range(16):
                total = total + p2_rcv[way, k * 2 + c].astype(F32)
            sums.append(total)
        for part in range(4):
            back.append(sums[part % 2][:, part // 2 * 512 : (part // 2 + 1) * 512])
    back = jnp.concatenate(back, axis=1) * sg[...].astype(F32).reshape(1, 4096)
    hat = s_ref[...].astype(F32) * stud_scale
    ig_ref[...] = stud_scale * (back - hat * jnp.mean(back * hat, axis=1, keepdims=True))
    add_loss(3)
    loss_ref[0, 0] = jnp.sum(jnp.where((sub == 0) & (lane == 0), ls_own[4], 0.0)) * (1.0 / 256)

    for out in outs:
        out.wait()
    left(s_snd.at[pl.ds(0, 7)], "spread")
    left(rows_a.at[0, pl.ds(0, 15)], "plane")
    left(rows_a.at[pl.ds(0, 3)], "ring")
    left(rows_a.at[pl.ds(0, 4)], "stud_side")
    left(gath.at[0, 0, pl.ds(0, 3), 0], "first")
    left(gath.at[0, pl.ds(0, 3), :, 0], "second")
    left(gath.at[pl.ds(0, 3), :, :, 0], "last")
    left(gath.at[:, :, :, 0], "side")
    left(st_rcv, "stats")
    left(ls_rcv.at[pl.ds(0, 10)], "loss")
    left(sib_snd, "sib")
    left(p1_snd.at[:, pl.ds(0, 3)], "line")
    left(p2_snd.at[:, pl.ds(0, 31)], "direct")
    for k, buf in enumerate((sl_snd, tl_snd, g_snd)):
        bulk_wait(buf, bulk_s, k)


def head_kernel(grad_hbm, rows_hbm, ig_hbm, out_hbm, ig_out, grad, rows, out, sems):
    move_ig = pltpu.make_async_copy(ig_hbm, ig_out, sems.at[17])
    move_ig.start()
    load_grad = pltpu.make_async_copy(grad_hbm, grad, sems.at[16])
    load_grad.start()
    loads, stores = [], []
    for j in range(8):
        loads.append(pltpu.make_async_copy(rows_hbm.at[j], rows.at[j], sems.at[j]))
        loads[j].start()
    load_grad.wait()
    for j in range(8):
        cols = pl.ds(j * 512, 512)
        loads[j].wait()
        out[:, cols] = jnp.dot(
            grad[...], rows[j].reshape(256, 512), preferred_element_type=F32
        ).astype(BF16)
        stores.append(pltpu.make_async_copy(out.at[:, cols], out_hbm.at[:, cols], sems.at[8 + j]))
        stores[j].start()
    for store in stores:
        store.wait()
    move_ig.wait()


def body(
    teacher_hidden,
    teacher_gain,
    teacher_head,
    student_hidden,
    student_gain,
    student_head,
    token_ids,
    teacher_map,
    student_map,
):
    vmem = pl.BlockSpec(memory_space=pltpu.VMEM)
    hbm = pl.BlockSpec(memory_space=pltpu.HBM)
    loss, input_grad, grad, rows = pl.pallas_call(
        kernel,
        out_shape=(
            jax.ShapeDtypeStruct((1, 1), F32),
            jax.ShapeDtypeStruct((2, 4096), F32),
            jax.ShapeDtypeStruct((512, 256), BF16),
            jax.ShapeDtypeStruct((8, 16, 16, 512), BF16),
        ),
        in_specs=[hbm] * 9,
        out_specs=(pl.BlockSpec(memory_space=pltpu.SMEM), vmem, hbm, hbm),
        scratch_shapes=[
            pltpu.VMEM((4, 4, 4, 2, 128, 256), BF16),
            pltpu.VMEM((512, 16384), BF16),
            pltpu.VMEM((512, 4096), BF16),
            pltpu.VMEM((16384,), BF16),
            pltpu.VMEM((4096,), BF16),
            pltpu.VMEM((2, 4096), BF16),
            pltpu.VMEM((128,), jnp.int32),
            pltpu.VMEM((128,), jnp.int32),
            pltpu.VMEM((8, 128), jnp.int32),
            pltpu.SMEM((256,), jnp.int32),
            pltpu.SMEM((8, 128), jnp.int32),
            pltpu.VMEM((256, 512), F32),
            pltpu.VMEM((256, 512), F32),
            pltpu.VMEM((8, 16, 16, 512), BF16),
            pltpu.VMEM((8, 2, 512), BF16),
            pltpu.VMEM((8, 2, 512), BF16),
            pltpu.VMEM((5, 2, 8, 128), F32),
            pltpu.VMEM((10, 2, 8, 128), F32),
            pltpu.VMEM((2, 128, 128), F32),
            pltpu.VMEM((128, 8, 128), BF16),
            pltpu.VMEM((128, 8, 128), BF16),
            pltpu.VMEM((128, 8, 128), BF16),
            pltpu.VMEM((128, 8, 128), BF16),
            pltpu.VMEM((128, 8, 128), BF16),
            pltpu.VMEM((128, 8, 128), BF16),
            pltpu.VMEM((256, 512), BF16),
            pltpu.VMEM((512, 256), BF16),
            pltpu.VMEM((4, 4, 4, 16, 512), BF16),
            pltpu.VMEM((4, 4, 4, 16, 512), BF16),
            pltpu.VMEM((4, 4, 4, 16, 512), F32),
            pltpu.VMEM((4, 4, 4, 16, 512), BF16),
            pltpu.VMEM((4, 3, 4, 16, 512), BF16),
            pltpu.VMEM((2, 32, 2, 1024), BF16),
            pltpu.VMEM((2, 32, 2, 1024), BF16),
            pltpu.VMEM((5, 8, 128), F32),
            pltpu.VMEM((13, 8, 128), F32),
            pltpu.SemaphoreType.DMA((len(SEND),)),
            pltpu.SemaphoreType.DMA((N_RECV,)),
            pltpu.SemaphoreType.DMA((12,)),
            pltpu.SemaphoreType.DMA((3,)),
            pltpu.SemaphoreType.DMA((3,)),
        ],
        compiler_params=pltpu.CompilerParams(
            collective_id=0, has_side_effects=True, vmem_limit_bytes=63 << 20
        ),
        cost_estimate=pl.CostEstimate(
            flops=2 * 256 * 512 * (16384 + 3 * 4096), bytes_accessed=24 << 20, transcendentals=0
        ),
        name="distill",
    )(
        teacher_hidden,
        teacher_gain,
        teacher_head,
        student_hidden,
        student_gain,
        student_head,
        token_ids,
        teacher_map,
        student_map,
    )
    head_grad, input_grad = pl.pallas_call(
        head_kernel,
        out_shape=(
            jax.ShapeDtypeStruct((512, 4096), BF16),
            jax.ShapeDtypeStruct((2, 4096), F32),
        ),
        in_specs=[hbm, hbm, hbm],
        out_specs=(hbm, hbm),
        scratch_shapes=[
            pltpu.VMEM((512, 256), BF16),
            pltpu.VMEM((8, 16, 16, 512), BF16),
            pltpu.VMEM((512, 4096), BF16),
            pltpu.SemaphoreType.DMA((18,)),
        ],
        compiler_params=pltpu.CompilerParams(vmem_limit_bytes=63 << 20),
        cost_estimate=pl.CostEstimate(
            flops=2 * 256 * 512 * 4096, bytes_accessed=6 << 20, transcendentals=0
        ),
        name="head",
    )(grad, rows, input_grad)
    return (loss.reshape(()), head_grad, input_grad)


def solution(mesh):
    placed = (
        P("role", "vocab"),
        P(),
        P(("role", "vocab"), None),
        P(("role", "vocab"), None),
        P(),
        P(("role", "vocab"), None),
        P(),
        P(),
        P(),
    )
    return jax.shard_map(
        body,
        mesh=mesh,
        in_specs=placed,
        out_specs=(P(), P(("role", "vocab"), None), P(("role", "vocab"), None)),
        check_vma=False,
    )
```
